32 devices in a mesh: groups: 2 (over y), ep: 16 (over z, x, core).
Axes of the slice: x: 2, y: 2, z: 4, core: 2. Of those that a mesh axis runs over, the one named last changes fastest.
Arguments:
- tokens: bfloat16 [4096, 7168], P(('groups', 'ep')), parts along dimension 0, may hold values from -6 to 6
- norm_gain: float32 [7168], replicated, may hold values from 0.1 to 1.9
- expert_gate: bfloat16 [7168, 16384], P(None, 'ep'), may hold values from -0.0625 to 0.0625
- expert_up: bfloat16 [7168, 16384], P(None, 'ep'), may hold values from -0.0625 to 0.0625
- expert_down: bfloat16 [16384, 7168], P('ep'), may hold values from -0.1875 to 0.1875
- route_ids: int32 [4096, 1], P(('groups', 'ep')), parts along dimension 0, may hold values from 0 to 15; in each aligned block of 128 rows (0 to 127, 128 to 255, ...) at most 8 rows name the same one
- route_gates: float32 [4096, 1], P(('groups', 'ep')), parts along dimension 0, may hold values from 0.1 to 1
Outputs:
- layer_out: bfloat16 [4096, 7168], P(('groups', 'ep')), parts along dimension 0
The draws below stay inside these ranges and needn't reach their ends.
There are 2 independent parts, one for each index of `groups`. The reference program is written for one: setup_inputs(seed, part) draws one part's arguments, and reference() takes and returns one part's arrays. A program takes and returns all parts, laid end to end along the dimension named above; an argument that names none is the same for every part. Nothing has to cross between parts.
Inputs may be any that keep to these rules, and one draw needn't show every extreme that they name: `route_ids`: among the rows of one device no expert is named by more than 8 routes, and in every draw some device names some expert exactly 8 times.
All inputs are finite; a program needn't handle non-finite values.
Results may differ from the reference program's by a relative error of at most 0.0042.
Values may be sent and summed in bfloat16 or wider, within the bound.
No kernel may reach another device: no remote copies, remote signals or barrier semaphores. Data moves between devices by JAX's collectives and lax.ppermute only.
A program may use at most 128 MiB of HBM per device.

```python
import math
import jax
import jax.numpy as jnp
import numpy as np
from jax import lax

D = 7168
ME = 1024
EXPERTS = 16
TOPK = 1
TOK_DEV = 128
TOKENS = 2048
SHARDS = 1
UNITS = 1024
CAP = 8


def levels(own_key, extent, split, least, high):
    def one(axis_at, shards_of):
        heights = jax.random.uniform(jax.random.fold_in(jax.random.fold_in(own_key, 6), axis_at), (shards_of,), jnp.float32, least / len(split), high / len(split))
        return jnp.repeat(jnp.exp(heights), extent[axis_at] // shards_of).reshape((-1,) + (1,) * (len(extent) - axis_at - 1))

    factor_of = one(*split[0])
    for cut in split[1:]:
        factor_of = factor_of * one(*cut)
    return factor_of


def routed_block(key, own, number, rows, count, top, most, skew):
    sequence = jax.random.permutation(key, count)
    heavy_load, common = load_shares(count, rows * top, most, skew, True), load_shares(count, rows * top, most, skew, False)
    places = jnp.arange(count)

    def named(sizes, turn):
        used = int((sizes > 0).sum())
        fixed = max(1, used // 4)
        moved = fixed + (places - fixed + turn * (used - fixed)) % max(1, count - fixed)
        return jnp.zeros((count,), jnp.int32).at[sequence[jnp.where(places < fixed, places, moved)]].set(jnp.asarray(sizes, jnp.int32))

    sizes = jnp.where(number % 4 == 0, named(heavy_load, number // 4), named(common, number - number // 4 - 1))
    mixed = jax.random.permutation(jax.random.fold_in(own, 3), count)
    donor, sink = mixed[0:count // 2 * 2:2], mixed[1:count // 2 * 2:2]
    margin = jnp.minimum(sizes[donor] - 1, most - sizes[sink]) // 2
    margin = jnp.where((donor == sequence[0]) | (sink == sequence[0]) | (sizes[sink] == 0), 0, jnp.maximum(margin, 0))
    moved = jax.random.randint(jax.random.fold_in(own, 4), (count // 2,), 0, 1 << 20) % (margin + 1)
    sizes = sizes.at[donor].add(-moved).at[sink].add(moved)
    labels = jnp.searchsorted(jnp.cumsum(sizes), jnp.arange(rows * top), side="right").astype(jnp.int32)
    table = labels.reshape(top, rows).T
    table = table[jax.random.permutation(jax.random.fold_in(own, 1), rows)]
    turn = jax.random.randint(jax.random.fold_in(own, 2), (rows, 1), 0, top)
    return jnp.take_along_axis(table, (jnp.arange(top)[None, :] + turn) % top, axis=1)


def load_shares(amount, total, most, skew, full):
    weights = [(1 << 20) // math.isqrt(grade ** skew) + 1 for grade in range(1, amount + 1)]
    largest = most if full else min(most, max(-(-total // amount), total * weights[0] // sum(weights)))
    least = 1 if total - largest >= amount - 1 else 0
    holding, spare = [largest] + [least] * (amount - 1), total - largest - least * (amount - 1)
    while spare > 0:
        candidates = [i for i in range(1, amount) if holding[i] < largest] or [i for i in range(1, amount) if holding[i] < most]
        pool, left = sum([weights[i] for i in candidates]), spare
        for i in candidates:
            extra = min(most - holding[i], max(1, left * weights[i] // pool), spare)
            holding[i] = holding[i] + extra
            spare = spare - extra
    return np.array(holding)


def normal_values(own_key, extent, spread, bound, cuts=(), kind=jnp.bfloat16):
    drawn = jax.random.normal(own_key, extent, jnp.float32) * spread
    if len(cuts) > 0:
        drawn = levels(own_key, extent, cuts, -0.22, 0.18) * drawn
    return jnp.clip(drawn, min=-bound, max=bound).astype(kind)


def setup_inputs(seed: int = 0, part: int = 0) -> dict:
    key_of = jax.random.split(jax.random.key(seed), 8)
    part_splits = jax.random.split(jax.random.fold_in(key_of[7], part), 8)
    tokens = normal_values(part_splits[0], (TOKENS, D), 1.0, 6.0, ((0, 16),))
    norm_gain = jnp.clip(1.0 + 0.18 * jax.random.normal(key_of[1], (D,), jnp.float32), 0.1, 1.9)
    expert_gate = normal_values(key_of[2], (D, EXPERTS * ME), D ** -0.5, 0.0625, ((1, 16),))
    expert_up = normal_values(key_of[3], (D, EXPERTS * ME), D ** -0.5, 0.0625, ((1, 16),))
    expert_down = normal_values(key_of[4], (EXPERTS * ME, D), ME ** -0.5, 0.1875, ((0, 16),))
    route_ids_keys = jax.random.split(jax.random.fold_in(part_splits[5], 1), TOKENS // TOK_DEV)
    route_ids_turns = jax.random.permutation(jax.random.fold_in(part_splits[5], 3), TOKENS // TOK_DEV)
    route_ids = jax.vmap(lambda own, number: routed_block(jax.random.fold_in(part_splits[5], 2), own, number, TOK_DEV, EXPERTS, TOPK, CAP, 2))(route_ids_keys, route_ids_turns).reshape((TOKENS, TOPK))
    route_gates = jnp.clip(jnp.exp(math.log(1.0) - 2.3025851 * jax.random.uniform(part_splits[6], (TOKENS, TOPK), jnp.float32) ** levels(part_splits[6], (TOKENS, TOPK), ((0, 16),), -0.2, 0.2)), 0.1, 1.0)
    return {"tokens": tokens, "norm_gain": norm_gain, "expert_gate": expert_gate, "expert_up": expert_up, "expert_down": expert_down, "route_ids": route_ids, "route_gates": route_gates}


def rms_scale(values, scale_gain):
    wide = values.astype(jnp.float32)
    mean_square = lax.optimization_barrier(jnp.mean(wide * wide, axis=-1, keepdims=True))
    return (wide * lax.rsqrt(mean_square + 1e-05) * scale_gain).astype(jnp.bfloat16)

def swiglu(inputs, w_gate, w_up):
    gate_proj = jnp.dot(inputs, w_gate, preferred_element_type=jnp.float32)
    up_proj = jnp.dot(inputs, w_up, preferred_element_type=jnp.float32)
    return (jax.nn.silu(gate_proj) * up_proj).astype(jnp.bfloat16)

def reference(tokens, norm_gain, expert_gate, expert_up, expert_down, route_ids, route_gates):
    normed = rms_scale(tokens, norm_gain)
    expert_match = (route_ids[:, :, None] == jnp.arange(EXPERTS, dtype=jnp.int32)[None, None, :]).astype(jnp.float32)
    weight = lax.optimization_barrier(jnp.sum(expert_match * route_gates[:, :, None], axis=1))
    routed = jnp.zeros((TOKENS, D), jnp.float32)
    for expert in range(EXPERTS):
        first = expert * ME
        expert_hidden = swiglu(normed, expert_gate[:, first:first + ME], expert_up[:, first:first + ME])
        part_sum = jnp.zeros((TOKENS, D), jnp.float32)
        for shard in range(SHARDS):
            lower = shard * UNITS
            part = jnp.dot(expert_hidden[:, lower:lower + UNITS], expert_down[first + lower:first + lower + UNITS], preferred_element_type=jnp.float32).astype(jnp.bfloat16)
            part_sum = part_sum + lax.optimization_barrier(part).astype(jnp.float32)
        routed = routed + weight[:, expert:expert + 1] * part_sum
    return (tokens.astype(jnp.float32) + routed).astype(jnp.bfloat16)
```

```python
import functools

import jax
import jax.numpy as jnp
from jax import lax
from jax.experimental import pallas as pl
from jax.experimental.pallas import tpu as pltpu
from jax.sharding import PartitionSpec as P

EXPERTS = 16
CAP = 8
PAIRS = EXPERTS // 2
GROUPS = ((4, 6, 0, 1, 2), (5, 7, 3))
RING = 3
SPLIT = 2
PREP_VMEM = 12 * 2**20
HBM = pl.BlockSpec(memory_space=pltpu.HBM)
VMEM = pl.BlockSpec(memory_space=pltpu.VMEM)


def tile_of(extent, most):
    size = min(most, extent)
    while extent % size:
        size -= 128
    return size


def turned(values, axis):
    count = max(values.shape)
    spread = jnp.broadcast_to(values, (count, count))
    row_at = lax.broadcasted_iota(jnp.int32, (count, count), 0)
    column_at = lax.broadcasted_iota(jnp.int32, (count, count), 1)
    return jnp.sum(jnp.where(row_at == column_at, spread, 0.0), axis=axis, keepdims=True)


def ranks(ids_row, axis):
    count = ids_row.shape[1]
    row_at = lax.broadcasted_iota(jnp.int32, (count, count), 0)
    column_at = lax.broadcasted_iota(jnp.int32, (count, count), 1)
    same = turned(ids_row, 1) == ids_row
    before = row_at < column_at if axis == 0 else column_at < row_at
    return jnp.sum(jnp.where(same & before, 1.0, 0.0), axis=axis, keepdims=True)


def prep_kernel(shards, tokens_hbm, gain_hbm, ids_hbm, gates_hbm, *refs):
    out_refs = refs[:PAIRS]
    slot_ref, gate_ref, tokens_ref, gain_ref, ids_ref, gates_ref, sems = refs[PAIRS:]
    count, width = tokens_ref.shape
    chunk = tile_of(width, 1024)
    starts = list(range(0, width, chunk))
    pairs = [(ids_hbm, ids_ref), (gates_hbm, gates_ref), (gain_hbm, gain_ref)]
    pairs += [(tokens_hbm.at[:, pl.ds(at, chunk)], tokens_ref.at[:, pl.ds(at, chunk)]) for at in starts]
    copies = [
        pltpu.make_async_copy(source, target, sems.at[i]) for i, (source, target) in enumerate(pairs)
    ]
    for copy in copies:
        copy.start()
    mine = lax.axis_index("ep") // shards
    copies[0].wait()
    ids_row = ids_ref[...]
    rank_row = ranks(ids_row.astype(jnp.float32), 0).astype(jnp.int32)
    slot_row = (ids_row ^ mine) * CAP + rank_row
    slots = EXPERTS * CAP
    pick = (lax.broadcasted_iota(jnp.int32, (slots, count), 0) == slot_row).astype(jnp.bfloat16)
    slot_ref[...] = jnp.broadcast_to(slot_row, slot_ref.shape)
    copies[1].wait()
    gate_ref[...] = jnp.broadcast_to(gates_ref[...], gate_ref.shape)
    square_sum = jnp.zeros((count, 128), jnp.float32)
    for first, copy in zip(starts, copies[3:]):
        copy.wait()
        for lane in range(first, first + chunk, 128):
            wide = tokens_ref[:, lane : lane + 128].astype(jnp.float32)
            square_sum = square_sum + wide * wide
    scale = lax.rsqrt(jnp.sum(square_sum, axis=1, keepdims=True) / width + 1e-05)
    copies[2].wait()
    for first in starts:
        part = slice(first, first + chunk)
        wide = tokens_ref[:, part].astype(jnp.float32)
        normed = (wide * scale * gain_ref[:, part]).astype(jnp.bfloat16)
        rows = jnp.dot(pick, normed, preferred_element_type=jnp.float32).astype(jnp.bfloat16)
        for k, out_ref in enumerate(out_refs):
            out_ref[:, part] = rows[k * 2 * CAP : (k + 1) * 2 * CAP]


def prepare(tokens, gain, ids, gates, shards):
    count, width = tokens.shape
    return pl.pallas_call(
        functools.partial(prep_kernel, shards),
        in_specs=[HBM] * 4,
        out_shape=[jax.ShapeDtypeStruct((2 * CAP, width), jnp.bfloat16)] * PAIRS
        + [
            jax.ShapeDtypeStruct((8, count), jnp.int32),
            jax.ShapeDtypeStruct((8, count), jnp.float32),
        ],
        scratch_shapes=[
            pltpu.VMEM((count, width), jnp.bfloat16),
            pltpu.VMEM((1, width), jnp.float32),
            pltpu.VMEM((1, count), jnp.int32),
            pltpu.VMEM((1, count), jnp.float32),
            pltpu.SemaphoreType.DMA((width // tile_of(width, 1024) + 3,)),
        ],
        compiler_params=pltpu.CompilerParams(vmem_limit_bytes=PREP_VMEM),
        cost_estimate=pl.CostEstimate(
            flops=2 * count * count * width, bytes_accessed=4 * count * width, transcendentals=0
        ),
        name="prepare",
    )(tokens, gain, ids, gates)


def halves_kernel(count, *refs):
    out_ref = refs[-1]
    width = out_ref.shape[1]
    chunk = tile_of(width, 1024)
    for first in range(0, width, chunk):
        part = slice(first, first + chunk)
        out_ref[:, part] = jnp.concatenate(
            [ref[:, part].astype(jnp.float32)[CAP:] for ref in refs[:count]], axis=0
        ).astype(jnp.bfloat16)


def second_halves(blocks, waits=()):
    width = blocks[0].shape[1]
    return pl.pallas_call(
        functools.partial(halves_kernel, len(blocks)),
        in_specs=[VMEM] * len(blocks) + [VMEM] * len(waits),
        out_specs=VMEM,
        out_shape=jax.ShapeDtypeStruct((CAP * len(blocks), width), jnp.bfloat16),
        compiler_params=pltpu.CompilerParams(vmem_limit_bytes=12 * 2**20),
        cost_estimate=pl.CostEstimate(
            flops=0, bytes_accessed=4 * CAP * len(blocks) * width, transcendentals=0
        ),
        name="second_halves",
    )(*blocks, *waits)


def zip_kernel(waits, upper_ref, lower_ref, *refs):
    out_refs = refs[waits:]
    width = upper_ref.shape[1]
    chunk = tile_of(width, 1024)
    for first in range(0, width, chunk):
        part = slice(first, first + chunk)
        upper = upper_ref[:, part].astype(jnp.float32)
        lower = lower_ref[:, part].astype(jnp.float32)
        for k, out_ref in enumerate(out_refs):
            rows = slice(k * CAP, (k + 1) * CAP)
            both = jnp.concatenate([upper[rows], lower[rows]], axis=0)
            out_ref[:, part] = both.astype(jnp.bfloat16)


def zipped(upper, lower, waits=()):
    rows, width = upper.shape
    return pl.pallas_call(
        functools.partial(zip_kernel, len(waits)),
        in_specs=[VMEM] * 2 + [VMEM] * len(waits),
        out_specs=[VMEM] * (rows // CAP),
        out_shape=[jax.ShapeDtypeStruct((2 * CAP, width), jnp.bfloat16)] * (rows // CAP),
        compiler_params=pltpu.CompilerParams(vmem_limit_bytes=12 * 2**20),
        cost_estimate=pl.CostEstimate(flops=0, bytes_accessed=8 * rows * width, transcendentals=0),
        name="zipped",
    )(upper, lower, *waits)


def after_kernel(count, *refs):
    for block_ref, out_ref in zip(refs[:count], refs[-count:]):
        out_ref[...] = block_ref[...]


def after(blocks, waits):
    count = len(blocks)
    return pl.pallas_call(
        functools.partial(after_kernel, count),
        in_specs=[VMEM] * (count + len(waits)),
        out_specs=[VMEM] * count,
        out_shape=[jax.ShapeDtypeStruct(block.shape, block.dtype) for block in blocks],
        compiler_params=pltpu.CompilerParams(vmem_limit_bytes=12 * 2**20),
        cost_estimate=pl.CostEstimate(flops=0, bytes_accessed=0, transcendentals=0),
        name="after",
    )(*blocks, *waits)


def ffn_kernel(takes, outs, gate_hbm, up_hbm, down_hbm, *refs):
    parts = len(takes)
    x_refs, out_refs = refs[:parts], refs[parts : parts + outs]
    x_all, gate_sum, up_sum, hidden, gate_ring, up_ring, down_ring, sems = refs[
        parts + outs :
    ]
    depth, columns = gate_ring.shape[1], down_ring.shape[2]
    width = x_all.shape[1]
    up_steps, down_steps = width // depth, width // columns
    ahead = min(RING, up_steps)
    down_ahead = min(RING, down_steps)

    def up_copies(step):
        slot = lax.rem(step, RING)
        share = depth // SPLIT
        copies = []
        for part in range(SPLIT):
            rows = pl.ds(pl.multiple_of(step * depth + part * share, share), share)
            to = pl.ds(part * share, share)
            for i, (hbm, ring) in enumerate(((gate_hbm, gate_ring), (up_hbm, up_ring))):
                copies.append(
                    pltpu.make_async_copy(hbm.at[rows], ring.at[slot, to], sems.at[i, slot, part])
                )
        return copies

    def down_copies(step):
        slot = lax.rem(step, RING)
        cols = pl.ds(pl.multiple_of(step * columns, columns), columns)
        share = down_ring.shape[1] // SPLIT
        return [
            pltpu.make_async_copy(
                down_hbm.at[pl.ds(part * share, share), cols],
                down_ring.at[slot, pl.ds(part * share, share)],
                sems.at[2, slot, part],
            )
            for part in range(SPLIT)
        ]

    for step in range(ahead):
        for copy in up_copies(step):
            copy.start()
    for step in range(down_ahead):
        for copy in down_copies(step):
            copy.start()
    for first in range(0, width, depth):
        x_all[:, first : first + depth] = jnp.concatenate(
            [
                ref[:, first : first + depth].astype(jnp.float32)[:take]
                for ref, take in zip(x_refs, takes)
            ],
            axis=0,
        ).astype(jnp.bfloat16)
    gate_sum[...] = jnp.zeros_like(gate_sum)
    up_sum[...] = jnp.zeros_like(up_sum)

    def up_step(step, carry):
        for copy in up_copies(step):
            copy.wait()
        slot = lax.rem(step, RING)
        x = x_all[:, pl.ds(pl.multiple_of(step * depth, depth), depth)]
        gate_sum[...] += jnp.dot(x, gate_ring[slot], preferred_element_type=jnp.float32)
        up_sum[...] += jnp.dot(x, up_ring[slot], preferred_element_type=jnp.float32)

        @pl.when(step + RING < up_steps)
        def _():
            for copy in up_copies(step + RING):
                copy.start()

        return carry

    lax.fori_loop(0, up_steps, up_step, 0)
    gate = gate_sum[...]
    hidden[...] = (gate / (1.0 + jnp.exp(-gate)) * up_sum[...]).astype(jnp.bfloat16)

    def down_step(step, carry):
        for copy in down_copies(step):
            copy.wait()
        part = jnp.dot(
            hidden[...], down_ring[lax.rem(step, RING)], preferred_element_type=jnp.float32
        )
        at = pl.ds(pl.multiple_of(step * columns, columns), columns)
        low = 0
        for out_ref in out_refs:
            rows = out_ref.shape[0]
            out_ref[:, at] = part[low : low + rows].astype(jnp.bfloat16)
            low += rows

        @pl.when(step + RING < down_steps)
        def _():
            for copy in down_copies(step + RING):
                copy.start()

        return carry

    lax.fori_loop(0, down_steps, down_step, 0)


def ffn(x_list, takes, out_rows, gate, up, down):
    parts = len(x_list)
    width = x_list[0].shape[1]
    units = gate.shape[1]
    depth = tile_of(width, 1024)
    columns = tile_of(width, 1024)
    total = sum(takes)
    return pl.pallas_call(
        functools.partial(ffn_kernel, takes, len(out_rows)),
        in_specs=[HBM] * 3 + [VMEM] * parts,
        out_specs=[VMEM] * len(out_rows),
        out_shape=[jax.ShapeDtypeStruct((rows, width), jnp.bfloat16) for rows in out_rows],
        scratch_shapes=[
            pltpu.VMEM((total, width), jnp.bfloat16),
            pltpu.VMEM((total, units), jnp.float32),
            pltpu.VMEM((total, units), jnp.float32),
            pltpu.VMEM((total, units), jnp.bfloat16),
            pltpu.VMEM((RING, depth, units), jnp.bfloat16),
            pltpu.VMEM((RING, depth, units), jnp.bfloat16),
            pltpu.VMEM((RING, units, columns), jnp.bfloat16),
            pltpu.SemaphoreType.DMA((3, RING, SPLIT)),
        ],
        compiler_params=pltpu.CompilerParams(vmem_limit_bytes=8 * 2**20 + 6 * RING * depth * units + 8 * total * width),
        cost_estimate=pl.CostEstimate(
            flops=6 * total * width * units,
            bytes_accessed=6 * width * units + 4 * total * width,
            transcendentals=total * units,
        ),
        name="ffn",
    )(gate, up, down, *x_list)


def combine_kernel(tokens_ref, slot_ref, gates_ref, *refs):
    back_refs, out_hbm, staged, sems = refs[:-3], refs[-3], refs[-2], refs[-1]
    count, width = tokens_ref.shape
    chunk = tile_of(width, 1024)
    slot = turned(slot_ref[0:1].astype(jnp.float32), 1).astype(jnp.int32)
    gates = turned(gates_ref[0:1], 1)
    slots = EXPERTS * CAP
    table = (lax.broadcasted_iota(jnp.int32, (count, slots), 1) == slot).astype(jnp.bfloat16)
    copies = []
    for i, first in enumerate(range(0, width, chunk)):
        part = slice(first, first + chunk)
        back = jnp.concatenate([ref[:, part] for ref in back_refs], axis=0)
        summed = jnp.dot(table, back, preferred_element_type=jnp.float32)
        wide = tokens_ref[:, part].astype(jnp.float32)
        staged[:, part] = (wide + gates * summed).astype(jnp.bfloat16)
        copies.append(
            pltpu.make_async_copy(
                staged.at[:, pl.ds(first, chunk)], out_hbm.at[:, pl.ds(first, chunk)], sems.at[i]
            )
        )
        copies[-1].start()
    for copy in copies:
        copy.wait()


def combine(tokens, slot_row, gates_row, back_list):
    count, width = tokens.shape
    return pl.pallas_call(
        combine_kernel,
        in_specs=[VMEM] * (3 + len(back_list)),
        out_specs=HBM,
        out_shape=jax.ShapeDtypeStruct((count, width), jnp.bfloat16),
        scratch_shapes=[
            pltpu.VMEM((count, width), jnp.bfloat16),
            pltpu.SemaphoreType.DMA((width // tile_of(width, 1024),)),
        ],
        compiler_params=pltpu.CompilerParams(vmem_limit_bytes=16 * 2**20),
        cost_estimate=pl.CostEstimate(
            flops=2 * count * count * width, bytes_accessed=6 * count * width, transcendentals=0
        ),
        name="combine",
    )(tokens, slot_row, gates_row, *back_list)


def per_device(tokens, norm_gain, expert_gate, expert_up, expert_down, route_ids, route_gates):
    devices = lax.axis_size("ep")
    shards = devices // EXPERTS
    count, width = tokens.shape
    weights = (expert_gate, expert_up, expert_down)
    holders = [[e * shards + s for s in range(shards)] for e in range(EXPERTS)]

    def across(block, k):
        if k == 0:
            return block
        pairs = [(d, (d // shards ^ k) * shards + d % shards) for d in range(devices)]
        return lax.ppermute(block, "ep", pairs)

    def expert(blocks, swapped):
        half = swapped.shape[0]
        takes = [CAP] * len(blocks) + [half]
        if shards == 1:
            return ffn(blocks + [swapped], takes, [half, half], *weights)
        rows = jnp.concatenate([block[:CAP] for block in blocks] + [swapped], axis=0)
        rows = lax.all_gather(rows, "ep", axis_index_groups=holders, tiled=True)
        (part,) = ffn([rows], [rows.shape[0]], [rows.shape[0]], *weights)
        part = lax.all_to_all(part, "ep", 0, 0, axis_index_groups=holders, tiled=True)
        part = part.reshape(shards, 2 * half, width).astype(jnp.float32)
        part = jnp.sum(part, axis=0).astype(jnp.bfloat16)
        return part[:half], part[half:]

    ids_row = route_ids.reshape(1, count)
    gates_row = route_gates.reshape(1, count)
    *sent, slot_row, gates_row = prepare(
        tokens, norm_gain.reshape(1, width), ids_row, gates_row, shards
    )
    early, late = GROUPS
    held = {m: across(sent[m], 2 * m) for m in early}
    later = after([sent[m] for m in late], [held[early[0]]])
    held.update({m: across(block, 2 * m) for m, block in zip(late, later)})
    back = {}
    for group in GROUPS:
        blocks = [held[m] for m in group]
        swapped = across(second_halves(blocks), 1)
        own, other = expert(blocks, swapped)
        waits = [held[m] for m in late] if group is early else [back[m] for m in early[:2]]
        (other,) = after([other], waits)
        blocks = dict(zip(group, zipped(own, across(other, 1))))
        if group is early:
            last = {m: blocks.pop(m) for m in early[2:]}
        else:
            near = [m for m in last if m]
            moved = after([last[m] for m in near], [blocks[late[0]]])
            blocks.update(zip(near, moved))
            blocks.update({m: block for m, block in last.items() if not m})
        back.update({m: across(block, 2 * m) for m, block in blocks.items()})
    return combine(tokens, slot_row, gates_row, [back[m] for m in range(PAIRS)])


def solution(mesh):
    in_specs = (
        P(("groups", "ep"), None),
        P(),
        P(None, "ep"),
        P(None, "ep"),
        P("ep", None),
        P(("groups", "ep"), None),
        P(("groups", "ep"), None),
    )
    out_specs = P(("groups", "ep"), None)
    return jax.shard_map(
        per_device, mesh=mesh, in_specs=in_specs, out_specs=out_specs, check_vma=False
    )
```

```python
import functools

import jax
import jax.numpy as jnp
from jax import lax
from jax.experimental import pallas as pl
from jax.experimental.pallas import tpu as pltpu
from jax.sharding import PartitionSpec as P

EXPERTS = 16
CAP = 8
PAIRS = EXPERTS // 2
PAIRED = ((4, 2, 1, 0), (5, 3))
SINGLE = ((12, 13), (14, 15))
BLOCKS = sorted(
    [(2 * m, 2, ("p", m)) for group in PAIRED for m in group]
    + [(k, 1, ("s", k)) for group in SINGLE for k in group]
)
FORWARD = (("p", 5), ("p", 3), ("s", 14), ("s", 15))
RETURN = (("p", 2), ("s", 12), ("p", 4))
RING = 3
SPLIT = 2
PREP_VMEM = 12 * 2**20
HBM = pl.BlockSpec(memory_space=pltpu.HBM)
VMEM = pl.BlockSpec(memory_space=pltpu.VMEM)


def tile_of(extent, most):
    size = min(most, extent)
    while extent % size:
        size -= 128
    return size


def turned(values, axis):
    count = max(values.shape)
    spread = jnp.broadcast_to(values, (count, count))
    row_at = lax.broadcasted_iota(jnp.int32, (count, count), 0)
    column_at = lax.broadcasted_iota(jnp.int32, (count, count), 1)
    return jnp.sum(jnp.where(row_at == column_at, spread, 0.0), axis=axis, keepdims=True)


def ranks(ids_row, axis):
    count = ids_row.shape[1]
    row_at = lax.broadcasted_iota(jnp.int32, (count, count), 0)
    column_at = lax.broadcasted_iota(jnp.int32, (count, count), 1)
    same = turned(ids_row, 1) == ids_row
    before = row_at < column_at if axis == 0 else column_at < row_at
    return jnp.sum(jnp.where(same & before, 1.0, 0.0), axis=axis, keepdims=True)


def prep_kernel(shards, tokens_hbm, gain_hbm, ids_hbm, gates_hbm, *refs):
    out_refs = refs[: len(BLOCKS)]
    slot_ref, gate_ref, tokens_ref, gain_ref, ids_ref, gates_ref, sems = refs[len(BLOCKS) :]
    count, width = tokens_ref.shape
    chunk = tile_of(width, 1024)
    starts = list(range(0, width, chunk))
    pairs = [(ids_hbm, ids_ref), (gates_hbm, gates_ref), (gain_hbm, gain_ref)]
    pairs += [(tokens_hbm.at[:, pl.ds(at, chunk)], tokens_ref.at[:, pl.ds(at, chunk)]) for at in starts]
    copies = [
        pltpu.make_async_copy(source, target, sems.at[i]) for i, (source, target) in enumerate(pairs)
    ]
    for copy in copies:
        copy.start()
    mine = lax.axis_index("ep") // shards
    copies[0].wait()
    ids_row = ids_ref[...]
    rank_row = ranks(ids_row.astype(jnp.float32), 0).astype(jnp.int32)
    slot_row = (ids_row ^ mine) * CAP + rank_row
    slots = EXPERTS * CAP
    pick = (lax.broadcasted_iota(jnp.int32, (slots, count), 0) == slot_row).astype(jnp.bfloat16)
    slot_ref[...] = jnp.broadcast_to(slot_row, slot_ref.shape)
    copies[1].wait()
    gate_ref[...] = jnp.broadcast_to(gates_ref[...], gate_ref.shape)
    square_sum = jnp.zeros((count, 128), jnp.float32)
    for first, copy in zip(starts, copies[3:]):
        copy.wait()
        for lane in range(first, first + chunk, 128):
            wide = tokens_ref[:, lane : lane + 128].astype(jnp.float32)
            square_sum = square_sum + wide * wide
    scale = lax.rsqrt(jnp.sum(square_sum, axis=1, keepdims=True) / width + 1e-05)
    copies[2].wait()
    for first in starts:
        part = slice(first, first + chunk)
        wide = tokens_ref[:, part].astype(jnp.float32)
        normed = (wide * scale * gain_ref[:, part]).astype(jnp.bfloat16)
        rows = jnp.dot(pick, normed, preferred_element_type=jnp.float32)
        for (k, size, _), out_ref in zip(BLOCKS, out_refs):
            out_ref[:, part] = rows[k * CAP : (k + size) * CAP].astype(jnp.bfloat16)


def prepare(tokens, gain, ids, gates, shards):
    count, width = tokens.shape
    return pl.pallas_call(
        functools.partial(prep_kernel, shards),
        in_specs=[HBM] * 4,
        out_shape=[
            jax.ShapeDtypeStruct((size * CAP, width), jnp.bfloat16) for _, size, _ in BLOCKS
        ]
        + [
            jax.ShapeDtypeStruct((8, count), jnp.int32),
            jax.ShapeDtypeStruct((8, count), jnp.float32),
        ],
        scratch_shapes=[
            pltpu.VMEM((count, width), jnp.bfloat16),
            pltpu.VMEM((1, width), jnp.float32),
            pltpu.VMEM((1, count), jnp.int32),
            pltpu.VMEM((1, count), jnp.float32),
            pltpu.SemaphoreType.DMA((width // tile_of(width, 1024) + 3,)),
        ],
        compiler_params=pltpu.CompilerParams(vmem_limit_bytes=PREP_VMEM),
        cost_estimate=pl.CostEstimate(
            flops=2 * count * count * width, bytes_accessed=4 * count * width, transcendentals=0
        ),
        name="prepare",
    )(tokens, gain, ids, gates)


def halves_kernel(count, *refs):
    out_ref = refs[-1]
    width = out_ref.shape[1]
    chunk = tile_of(width, 1024)
    for first in range(0, width, chunk):
        part = slice(first, first + chunk)
        out_ref[:, part] = jnp.concatenate(
            [ref[:, part].astype(jnp.float32)[CAP:] for ref in refs[:count]], axis=0
        ).astype(jnp.bfloat16)


def second_halves(blocks, waits=()):
    width = blocks[0].shape[1]
    return pl.pallas_call(
        functools.partial(halves_kernel, len(blocks)),
        in_specs=[VMEM] * len(blocks) + [VMEM] * len(waits),
        out_specs=VMEM,
        out_shape=jax.ShapeDtypeStruct((CAP * len(blocks), width), jnp.bfloat16),
        compiler_params=pltpu.CompilerParams(vmem_limit_bytes=12 * 2**20),
        cost_estimate=pl.CostEstimate(
            flops=0, bytes_accessed=4 * CAP * len(blocks) * width, transcendentals=0
        ),
        name="second_halves",
    )(*blocks, *waits)


def zip_kernel(waits, upper_ref, lower_ref, *refs):
    out_refs = refs[waits:]
    width = upper_ref.shape[1]
    chunk = tile_of(width, 1024)
    for first in range(0, width, chunk):
        part = slice(first, first + chunk)
        upper = upper_ref[:, part].astype(jnp.float32)
        lower = lower_ref[:, part].astype(jnp.float32)
        for k, out_ref in enumerate(out_refs):
            rows = slice(k * CAP, (k + 1) * CAP)
            both = jnp.concatenate([upper[rows], lower[rows]], axis=0)
            out_ref[:, part] = both.astype(jnp.bfloat16)


def zipped(upper, lower, waits=()):
    rows, width = upper.shape
    return pl.pallas_call(
        functools.partial(zip_kernel, len(waits)),
        in_specs=[VMEM] * 2 + [VMEM] * len(waits),
        out_specs=[VMEM] * (rows // CAP),
        out_shape=[jax.ShapeDtypeStruct((2 * CAP, width), jnp.bfloat16)] * (rows // CAP),
        compiler_params=pltpu.CompilerParams(vmem_limit_bytes=12 * 2**20),
        cost_estimate=pl.CostEstimate(flops=0, bytes_accessed=8 * rows * width, transcendentals=0),
        name="zipped",
    )(upper, lower, *waits)


def after_kernel(count, *refs):
    for block_ref, out_ref in zip(refs[:count], refs[-count:]):
        out_ref[...] = block_ref[...]


def after(blocks, waits):
    count = len(blocks)
    return pl.pallas_call(
        functools.partial(after_kernel, count),
        in_specs=[VMEM] * (count + len(waits)),
        out_specs=[VMEM] * count,
        out_shape=[jax.ShapeDtypeStruct(block.shape, block.dtype) for block in blocks],
        compiler_params=pltpu.CompilerParams(vmem_limit_bytes=12 * 2**20),
        cost_estimate=pl.CostEstimate(flops=0, bytes_accessed=0, transcendentals=0),
        name="after",
    )(*blocks, *waits)


def ffn_kernel(takes, outs, gate_hbm, up_hbm, down_hbm, *refs):
    parts = len(takes)
    x_refs, out_refs = refs[:parts], refs[parts : parts + outs]
    x_all, gate_sum, up_sum, hidden, gate_ring, up_ring, down_ring, sems = refs[
        parts + outs :
    ]
    depth, columns = gate_ring.shape[1], down_ring.shape[2]
    width = x_all.shape[1]
    up_steps, down_steps = width // depth, width // columns
    ahead = min(RING, up_steps)
    down_ahead = min(RING, down_steps)

    def up_copies(step):
        slot = lax.rem(step, RING)
        share = depth // SPLIT
        copies = []
        for part in range(SPLIT):
            rows = pl.ds(pl.multiple_of(step * depth + part * share, share), share)
            to = pl.ds(part * share, share)
            for i, (hbm, ring) in enumerate(((gate_hbm, gate_ring), (up_hbm, up_ring))):
                copies.append(
                    pltpu.make_async_copy(hbm.at[rows], ring.at[slot, to], sems.at[i, slot, part])
                )
        return copies

    def down_copies(step):
        slot = lax.rem(step, RING)
        cols = pl.ds(pl.multiple_of(step * columns, columns), columns)
        share = down_ring.shape[1] // SPLIT
        return [
            pltpu.make_async_copy(
                down_hbm.at[pl.ds(part * share, share), cols],
                down_ring.at[slot, pl.ds(part * share, share)],
                sems.at[2, slot, part],
            )
            for part in range(SPLIT)
        ]

    for step in range(ahead):
        for copy in up_copies(step):
            copy.start()
    for step in range(down_ahead):
        for copy in down_copies(step):
            copy.start()
    for first in range(0, width, depth):
        x_all[:, first : first + depth] = jnp.concatenate(
            [
                ref[:, first : first + depth].astype(jnp.float32)[:take]
                for ref, take in zip(x_refs, takes)
            ],
            axis=0,
        ).astype(jnp.bfloat16)
    gate_sum[...] = jnp.zeros_like(gate_sum)
    up_sum[...] = jnp.zeros_like(up_sum)

    def up_step(step, carry):
        for copy in up_copies(step):
            copy.wait()
        slot = lax.rem(step, RING)
        x = x_all[:, pl.ds(pl.multiple_of(step * depth, depth), depth)]
        gate_sum[...] += jnp.dot(x, gate_ring[slot], preferred_element_type=jnp.float32)
        up_sum[...] += jnp.dot(x, up_ring[slot], preferred_element_type=jnp.float32)

        @pl.when(step + RING < up_steps)
        def _():
            for copy in up_copies(step + RING):
                copy.start()

        return carry

    lax.fori_loop(0, up_steps, up_step, 0)
    gate = gate_sum[...]
    hidden[...] = (gate / (1.0 + jnp.exp(-gate)) * up_sum[...]).astype(jnp.bfloat16)

    def down_step(step, carry):
        for copy in down_copies(step):
            copy.wait()
        part = jnp.dot(
            hidden[...], down_ring[lax.rem(step, RING)], preferred_element_type=jnp.float32
        )
        at = pl.ds(pl.multiple_of(step * columns, columns), columns)
        low = 0
        for out_ref in out_refs:
            rows = out_ref.shape[0]
            out_ref[:, at] = part[low : low + rows].astype(jnp.bfloat16)
            low += rows

        @pl.when(step + RING < down_steps)
        def _():
            for copy in down_copies(step + RING):
                copy.start()

        return carry

    lax.fori_loop(0, down_steps, down_step, 0)


def ffn(x_list, takes, out_rows, gate, up, down):
    parts = len(x_list)
    width = x_list[0].shape[1]
    units = gate.shape[1]
    depth = tile_of(width, 1024)
    columns = tile_of(width, 1024)
    total = sum(takes)
    return pl.pallas_call(
        functools.partial(ffn_kernel, takes, len(out_rows)),
        in_specs=[HBM] * 3 + [VMEM] * parts,
        out_specs=[VMEM] * len(out_rows),
        out_shape=[jax.ShapeDtypeStruct((rows, width), jnp.bfloat16) for rows in out_rows],
        scratch_shapes=[
            pltpu.VMEM((total, width), jnp.bfloat16),
            pltpu.VMEM((total, units), jnp.float32),
            pltpu.VMEM((total, units), jnp.float32),
            pltpu.VMEM((total, units), jnp.bfloat16),
            pltpu.VMEM((RING, depth, units), jnp.bfloat16),
            pltpu.VMEM((RING, depth, units), jnp.bfloat16),
            pltpu.VMEM((RING, units, columns), jnp.bfloat16),
            pltpu.SemaphoreType.DMA((3, RING, SPLIT)),
        ],
        compiler_params=pltpu.CompilerParams(vmem_limit_bytes=50 * 2**20),
        cost_estimate=pl.CostEstimate(
            flops=6 * total * width * units,
            bytes_accessed=6 * width * units + 4 * total * width,
            transcendentals=total * units,
        ),
        name="ffn",
    )(gate, up, down, *x_list)


def combine_kernel(tokens_ref, slot_ref, gates_ref, *refs):
    back_refs, out_hbm, staged, sems = refs[:-3], refs[-3], refs[-2], refs[-1]
    count, width = tokens_ref.shape
    chunk = tile_of(width, 1024)
    slot = turned(slot_ref[0:1].astype(jnp.float32), 1).astype(jnp.int32)
    gates = turned(gates_ref[0:1], 1)
    slots = EXPERTS * CAP
    table = (lax.broadcasted_iota(jnp.int32, (count, slots), 1) == slot).astype(jnp.bfloat16)
    copies = []
    for i, first in enumerate(range(0, width, chunk)):
        part = slice(first, first + chunk)
        back = jnp.concatenate(
            [ref[:, part].astype(jnp.float32) for ref in back_refs], axis=0
        ).astype(jnp.bfloat16)
        summed = jnp.dot(table, back, preferred_element_type=jnp.float32)
        wide = tokens_ref[:, part].astype(jnp.float32)
        staged[:, part] = (wide + gates * summed).astype(jnp.bfloat16)
        copies.append(
            pltpu.make_async_copy(
                staged.at[:, pl.ds(first, chunk)], out_hbm.at[:, pl.ds(first, chunk)], sems.at[i]
            )
        )
        copies[-1].start()
    for copy in copies:
        copy.wait()


def combine(tokens, slot_row, gates_row, back_list):
    count, width = tokens.shape
    return pl.pallas_call(
        combine_kernel,
        in_specs=[VMEM] * (3 + len(back_list)),
        out_specs=HBM,
        out_shape=jax.ShapeDtypeStruct((count, width), jnp.bfloat16),
        scratch_shapes=[
            pltpu.VMEM((count, width), jnp.bfloat16),
            pltpu.SemaphoreType.DMA((width // tile_of(width, 1024),)),
        ],
        compiler_params=pltpu.CompilerParams(vmem_limit_bytes=16 * 2**20),
        cost_estimate=pl.CostEstimate(
            flops=2 * count * count * width, bytes_accessed=6 * count * width, transcendentals=0
        ),
        name="combine",
    )(tokens, slot_row, gates_row, *back_list)


def per_device(tokens, norm_gain, expert_gate, expert_up, expert_down, route_ids, route_gates):
    devices = lax.axis_size("ep")
    shards = devices // EXPERTS
    count, width = tokens.shape
    weights = (expert_gate, expert_up, expert_down)
    holders = [[e * shards + s for s in range(shards)] for e in range(EXPERTS)]

    def across(block, k):
        if k == 0:
            return block
        pairs = [(d, (d // shards ^ k) * shards + d % shards) for d in range(devices)]
        return lax.ppermute(block, "ep", pairs)

    def expert(pairs, swapped, singles):
        half = swapped.shape[0]
        x_list = pairs + [swapped] + singles
        takes = [CAP] * len(pairs) + [half] + [CAP] * len(singles)
        out_rows = [half, half] + [CAP] * len(singles)
        if shards == 1:
            return ffn(x_list, takes, out_rows, *weights)
        rows = jnp.concatenate([x[:take] for x, take in zip(x_list, takes)], axis=0)
        rows = lax.all_gather(rows, "ep", axis_index_groups=holders, tiled=True)
        (part,) = ffn([rows], [rows.shape[0]], [rows.shape[0]], *weights)
        part = lax.all_to_all(part, "ep", 0, 0, axis_index_groups=holders, tiled=True)
        part = part.reshape(shards, -1, width).astype(jnp.float32)
        part = jnp.sum(part, axis=0).astype(jnp.bfloat16)
        return jnp.split(part, [sum(out_rows[: i + 1]) for i in range(len(out_rows) - 1)], axis=0)

    ids_row = route_ids.reshape(1, count)
    gates_row = route_gates.reshape(1, count)
    *sent, slot_row, gates_row = prepare(
        tokens, norm_gain.reshape(1, width), ids_row, gates_row, shards
    )
    sent = {name: block for (_, _, name), block in zip(BLOCKS, sent)}

    def move(name, block):
        return across(block, 2 * name[1] if name[0] == "p" else name[1])

    early, late = (
        [("p", m) for m in pairs] + [("s", k) for k in singles]
        for pairs, singles in zip(PAIRED, SINGLE)
    )
    held = {name: move(name, sent[name]) for name in early}
    later = after([sent[name] for name in late], [held[early[0]]])
    held.update({name: move(name, block) for name, block in zip(late, later)})
    back = {}
    for group in (early, late):
        pairs = [name for name in group if name[0] == "p"]
        singles = [name for name in group if name[0] == "s"]
        blocks = [held[name] for name in pairs]
        first = [held[name] for name in singles] if group is early else []
        swapped = across(second_halves(blocks, first), 1)
        own, other, *results = expert(blocks, swapped, [held[name] for name in singles])
        waits = [held[name] for name in FORWARD] if group is early else [back[name] for name in RETURN]
        if group is early:
            (other,) = after([other], waits)
        else:
            other, *results = after([other] + results, waits)
        blocks = dict(zip(singles, results))
        blocks.update(zip(pairs, zipped(own, across(other, 1))))
        back.update({name: move(name, blocks[name]) for name in group})
    return combine(tokens, slot_row, gates_row, [back[name] for _, _, name in BLOCKS])


def solution(mesh):
    in_specs = (
        P(("groups", "ep"), None),
        P(),
        P(None, "ep"),
        P(None, "ep"),
        P("ep", None),
        P(("groups", "ep"), None),
        P(("groups", "ep"), None),
    )
    out_specs = P(("groups", "ep"), None)
    return jax.shard_map(
        per_device, mesh=mesh, in_specs=in_specs, out_specs=out_specs, check_vma=False
    )
```

```python
import functools

import jax
import jax.numpy as jnp
from jax import lax
from jax.experimental import pallas as pl
from jax.experimental.pallas import tpu as pltpu
from jax.sharding import PartitionSpec as P

EXPERTS = 16
CAP = 8
PAIRS = EXPERTS // 2
PAIRED = ((4, 2, 1, 0), (5, 3))
SINGLE = ((12, 13), (14, 15))
BLOCKS = sorted(
    [(2 * m, 2, ("p", m)) for group in PAIRED for m in group]
    + [(k, 1, ("s", k)) for group in SINGLE for k in group]
)
FORWARD = (("p", 5), ("p", 3), ("s", 14), ("s", 15))
RETURN = (("p", 2), ("s", 12), ("p", 4))
RING = 3
SPLIT = 2
PREP_VMEM = 51 * 2**20
HBM = pl.BlockSpec(memory_space=pltpu.HBM)
VMEM = pl.BlockSpec(memory_space=pltpu.VMEM)


def tile_of(extent, most):
    size = min(most, extent)
    while extent % size:
        size -= 128
    return size


def turned(values, axis):
    count = max(values.shape)
    spread = jnp.broadcast_to(values, (count, count))
    row_at = lax.broadcasted_iota(jnp.int32, (count, count), 0)
    column_at = lax.broadcasted_iota(jnp.int32, (count, count), 1)
    return jnp.sum(jnp.where(row_at == column_at, spread, 0.0), axis=axis, keepdims=True)


def ranks(ids_row, axis):
    count = ids_row.shape[1]
    row_at = lax.broadcasted_iota(jnp.int32, (count, count), 0)
    column_at = lax.broadcasted_iota(jnp.int32, (count, count), 1)
    same = turned(ids_row, 1) == ids_row
    before = row_at < column_at if axis == 0 else column_at < row_at
    return jnp.sum(jnp.where(same & before, 1.0, 0.0), axis=axis, keepdims=True)


def prep_kernel(shards, tokens_hbm, vectors_ref, *refs):
    out_refs = refs[: len(BLOCKS)]
    slot_ref, gate_ref, tokens_ref, sems = refs[len(BLOCKS) :]
    count, width = tokens_ref.shape
    chunk = tile_of(width, 1024)
    starts = list(range(0, width, chunk))
    copies = [
        pltpu.make_async_copy(
            tokens_hbm.at[:, pl.ds(at, chunk)], tokens_ref.at[:, pl.ds(at, chunk)], sems.at[i]
        )
        for i, at in enumerate(starts)
    ]
    for copy in copies:
        copy.start()
    mine = lax.axis_index("ep") // shards
    ids_row = vectors_ref[:, width : width + count].astype(jnp.int32)
    rank_row = ranks(ids_row.astype(jnp.float32), 0).astype(jnp.int32)
    slot_row = (ids_row ^ mine) * CAP + rank_row
    slots = EXPERTS * CAP
    pick = (lax.broadcasted_iota(jnp.int32, (slots, count), 0) == slot_row).astype(jnp.bfloat16)
    slot_ref[...] = jnp.broadcast_to(slot_row, slot_ref.shape)
    gate_ref[...] = jnp.broadcast_to(vectors_ref[:, width + count :], gate_ref.shape)
    square_sum = jnp.zeros((count, 128), jnp.float32)
    for first, copy in zip(starts, copies):
        copy.wait()
        for lane in range(first, first + chunk, 128):
            wide = tokens_ref[:, lane : lane + 128].astype(jnp.float32)
            square_sum = square_sum + wide * wide
    scale = lax.rsqrt(jnp.sum(square_sum, axis=1, keepdims=True) / width + 1e-05)
    for first in starts:
        part = slice(first, first + chunk)
        wide = tokens_ref[:, part].astype(jnp.float32)
        normed = (wide * scale * vectors_ref[:, part]).astype(jnp.bfloat16)
        rows = jnp.dot(pick, normed, preferred_element_type=jnp.float32)
        for (k, size, _), out_ref in zip(BLOCKS, out_refs):
            out_ref[:, part] = rows[k * CAP : (k + size) * CAP].astype(jnp.bfloat16)


def prepare(tokens, vectors, shards):
    count, width = tokens.shape
    return pl.pallas_call(
        functools.partial(prep_kernel, shards),
        in_specs=[HBM, VMEM],
        out_shape=[
            jax.ShapeDtypeStruct((size * CAP, width), jnp.bfloat16) for _, size, _ in BLOCKS
        ]
        + [
            jax.ShapeDtypeStruct((8, count), jnp.int32),
            jax.ShapeDtypeStruct((8, count), jnp.float32),
        ],
        scratch_shapes=[
            pltpu.VMEM((count, width), jnp.bfloat16),
            pltpu.SemaphoreType.DMA((width // tile_of(width, 1024),)),
        ],
        compiler_params=pltpu.CompilerParams(vmem_limit_bytes=PREP_VMEM),
        cost_estimate=pl.CostEstimate(
            flops=2 * count * count * width, bytes_accessed=4 * count * width, transcendentals=0
        ),
        name="prepare",
    )(tokens, vectors)


def halves_kernel(count, *refs):
    out_ref = refs[-1]
    width = out_ref.shape[1]
    chunk = tile_of(width, 1024)
    for first in range(0, width, chunk):
        part = slice(first, first + chunk)
        out_ref[:, part] = jnp.concatenate(
            [ref[:, part].astype(jnp.float32)[CAP:] for ref in refs[:count]], axis=0
        ).astype(jnp.bfloat16)


def second_halves(blocks, waits=()):
    width = blocks[0].shape[1]
    return pl.pallas_call(
        functools.partial(halves_kernel, len(blocks)),
        in_specs=[VMEM] * len(blocks) + [VMEM] * len(waits),
        out_specs=VMEM,
        out_shape=jax.ShapeDtypeStruct((CAP * len(blocks), width), jnp.bfloat16),
        compiler_params=pltpu.CompilerParams(vmem_limit_bytes=12 * 2**20),
        cost_estimate=pl.CostEstimate(
            flops=0, bytes_accessed=4 * CAP * len(blocks) * width, transcendentals=0
        ),
        name="second_halves",
    )(*blocks, *waits)


def zip_kernel(waits, upper_ref, lower_ref, *refs):
    out_refs = refs[waits:]
    width = upper_ref.shape[1]
    chunk = tile_of(width, 1024)
    for first in range(0, width, chunk):
        part = slice(first, first + chunk)
        upper = upper_ref[:, part].astype(jnp.float32)
        lower = lower_ref[:, part].astype(jnp.float32)
        for k, out_ref in enumerate(out_refs):
            rows = slice(k * CAP, (k + 1) * CAP)
            both = jnp.concatenate([upper[rows], lower[rows]], axis=0)
            out_ref[:, part] = both.astype(jnp.bfloat16)


def zipped(upper, lower, waits=()):
    rows, width = upper.shape
    return pl.pallas_call(
        functools.partial(zip_kernel, len(waits)),
        in_specs=[VMEM] * 2 + [VMEM] * len(waits),
        out_specs=[VMEM] * (rows // CAP),
        out_shape=[jax.ShapeDtypeStruct((2 * CAP, width), jnp.bfloat16)] * (rows // CAP),
        compiler_params=pltpu.CompilerParams(vmem_limit_bytes=12 * 2**20),
        cost_estimate=pl.CostEstimate(flops=0, bytes_accessed=8 * rows * width, transcendentals=0),
        name="zipped",
    )(upper, lower, *waits)


def after_kernel(count, *refs):
    for block_ref, out_ref in zip(refs[:count], refs[-count:]):
        out_ref[...] = block_ref[...]


def after(blocks, waits):
    count = len(blocks)
    return pl.pallas_call(
        functools.partial(after_kernel, count),
        in_specs=[VMEM] * (count + len(waits)),
        out_specs=[VMEM] * count,
        out_shape=[jax.ShapeDtypeStruct(block.shape, block.dtype) for block in blocks],
        compiler_params=pltpu.CompilerParams(vmem_limit_bytes=12 * 2**20),
        cost_estimate=pl.CostEstimate(flops=0, bytes_accessed=0, transcendentals=0),
        name="after",
    )(*blocks, *waits)


def ffn_kernel(takes, outs, gate_hbm, up_hbm, down_hbm, *refs):
    parts = len(takes)
    x_refs, out_refs = refs[:parts], refs[parts : parts + outs]
    x_all, gate_sum, up_sum, hidden, gate_ring, up_ring, down_ring, sems = refs[
        parts + outs :
    ]
    depth, columns = gate_ring.shape[1], down_ring.shape[2]
    width = x_all.shape[1]
    up_steps, down_steps = width // depth, width // columns
    ahead = min(RING, up_steps)
    down_ahead = min(RING, down_steps)

    def up_copies(step):
        slot = lax.rem(step, RING)
        share = depth // SPLIT
        copies = []
        for part in range(SPLIT):
            rows = pl.ds(pl.multiple_of(step * depth + part * share, share), share)
            to = pl.ds(part * share, share)
            for i, (hbm, ring) in enumerate(((gate_hbm, gate_ring), (up_hbm, up_ring))):
                copies.append(
                    pltpu.make_async_copy(hbm.at[rows], ring.at[slot, to], sems.at[i, slot, part])
                )
        return copies

    def down_copies(step):
        slot = lax.rem(step, RING)
        cols = pl.ds(pl.multiple_of(step * columns, columns), columns)
        share = down_ring.shape[1] // SPLIT
        return [
            pltpu.make_async_copy(
                down_hbm.at[pl.ds(part * share, share), cols],
                down_ring.at[slot, pl.ds(part * share, share)],
                sems.at[2, slot, part],
            )
            for part in range(SPLIT)
        ]

    for step in range(ahead):
        for copy in up_copies(step):
            copy.start()
    for step in range(down_ahead):
        for copy in down_copies(step):
            copy.start()
    for first in range(0, width, depth):
        x_all[:, first : first + depth] = jnp.concatenate(
            [
                ref[:, first : first + depth].astype(jnp.float32)[:take]
                for ref, take in zip(x_refs, takes)
            ],
            axis=0,
        ).astype(jnp.bfloat16)
    gate_sum[...] = jnp.zeros_like(gate_sum)
    up_sum[...] = jnp.zeros_like(up_sum)

    def up_step(step, carry):
        for copy in up_copies(step):
            copy.wait()
        slot = lax.rem(step, RING)
        x = x_all[:, pl.ds(pl.multiple_of(step * depth, depth), depth)]
        gate_sum[...] += jnp.dot(x, gate_ring[slot], preferred_element_type=jnp.float32)
        up_sum[...] += jnp.dot(x, up_ring[slot], preferred_element_type=jnp.float32)

        @pl.when(step + RING < up_steps)
        def _():
            for copy in up_copies(step + RING):
                copy.start()

        return carry

    lax.fori_loop(0, up_steps, up_step, 0)
    gate = gate_sum[...]
    hidden[...] = (gate / (1.0 + jnp.exp(-gate)) * up_sum[...]).astype(jnp.bfloat16)

    def down_step(step, carry):
        for copy in down_copies(step):
            copy.wait()
        part = jnp.dot(
            hidden[...], down_ring[lax.rem(step, RING)], preferred_element_type=jnp.float32
        )
        at = pl.ds(pl.multiple_of(step * columns, columns), columns)
        low = 0
        for out_ref in out_refs:
            rows = out_ref.shape[0]
            out_ref[:, at] = part[low : low + rows].astype(jnp.bfloat16)
            low += rows

        @pl.when(step + RING < down_steps)
        def _():
            for copy in down_copies(step + RING):
                copy.start()

        return carry

    lax.fori_loop(0, down_steps, down_step, 0)


def ffn(x_list, takes, out_rows, gate, up, down):
    parts = len(x_list)
    width = x_list[0].shape[1]
    units = gate.shape[1]
    depth = tile_of(width, 1024)
    columns = tile_of(width, 1024)
    total = sum(takes)
    return pl.pallas_call(
        functools.partial(ffn_kernel, takes, len(out_rows)),
        in_specs=[HBM] * 3 + [VMEM] * parts,
        out_specs=[VMEM] * len(out_rows),
        out_shape=[jax.ShapeDtypeStruct((rows, width), jnp.bfloat16) for rows in out_rows],
        scratch_shapes=[
            pltpu.VMEM((total, width), jnp.bfloat16),
            pltpu.VMEM((total, units), jnp.float32),
            pltpu.VMEM((total, units), jnp.float32),
            pltpu.VMEM((total, units), jnp.bfloat16),
            pltpu.VMEM((RING, depth, units), jnp.bfloat16),
            pltpu.VMEM((RING, depth, units), jnp.bfloat16),
            pltpu.VMEM((RING, units, columns), jnp.bfloat16),
            pltpu.SemaphoreType.DMA((3, RING, SPLIT)),
        ],
        compiler_params=pltpu.CompilerParams(vmem_limit_bytes=50 * 2**20),
        cost_estimate=pl.CostEstimate(
            flops=6 * total * width * units,
            bytes_accessed=6 * width * units + 4 * total * width,
            transcendentals=total * units,
        ),
        name="ffn",
    )(gate, up, down, *x_list)


def combine_kernel(tokens_ref, slot_ref, gates_ref, *refs):
    back_refs, out_hbm, staged, sems = refs[:-3], refs[-3], refs[-2], refs[-1]
    count, width = tokens_ref.shape
    chunk = tile_of(width, 1024)
    slot = turned(slot_ref[0:1].astype(jnp.float32), 1).astype(jnp.int32)
    gates = turned(gates_ref[0:1], 1)
    slots = EXPERTS * CAP
    table = (lax.broadcasted_iota(jnp.int32, (count, slots), 1) == slot).astype(jnp.bfloat16)
    copies = []
    for i, first in enumerate(range(0, width, chunk)):
        part = slice(first, first + chunk)
        back = jnp.concatenate(
            [ref[:, part].astype(jnp.float32) for ref in back_refs], axis=0
        ).astype(jnp.bfloat16)
        summed = jnp.dot(table, back, preferred_element_type=jnp.float32)
        wide = tokens_ref[:, part].astype(jnp.float32)
        staged[:, part] = (wide + gates * summed).astype(jnp.bfloat16)
        copies.append(
            pltpu.make_async_copy(
                staged.at[:, pl.ds(first, chunk)], out_hbm.at[:, pl.ds(first, chunk)], sems.at[i]
            )
        )
        copies[-1].start()
    for copy in copies:
        copy.wait()


def combine(tokens, slot_row, gates_row, back_list):
    count, width = tokens.shape
    return pl.pallas_call(
        combine_kernel,
        in_specs=[VMEM] * (3 + len(back_list)),
        out_specs=HBM,
        out_shape=jax.ShapeDtypeStruct((count, width), jnp.bfloat16),
        scratch_shapes=[
            pltpu.VMEM((count, width), jnp.bfloat16),
            pltpu.SemaphoreType.DMA((width // tile_of(width, 1024),)),
        ],
        compiler_params=pltpu.CompilerParams(vmem_limit_bytes=16 * 2**20),
        cost_estimate=pl.CostEstimate(
            flops=2 * count * count * width, bytes_accessed=6 * count * width, transcendentals=0
        ),
        name="combine",
    )(tokens, slot_row, gates_row, *back_list)


def per_device(tokens, norm_gain, expert_gate, expert_up, expert_down, route_ids, route_gates):
    devices = lax.axis_size("ep")
    shards = devices // EXPERTS
    count, width = tokens.shape
    weights = (expert_gate, expert_up, expert_down)
    holders = [[e * shards + s for s in range(shards)] for e in range(EXPERTS)]

    def across(block, k):
        if k == 0:
            return block
        pairs = [(d, (d // shards ^ k) * shards + d % shards) for d in range(devices)]
        return lax.ppermute(block, "ep", pairs)

    def expert(pairs, swapped, singles):
        half = swapped.shape[0]
        x_list = pairs + [swapped] + singles
        takes = [CAP] * len(pairs) + [half] + [CAP] * len(singles)
        out_rows = [half, half] + [CAP] * len(singles)
        if shards == 1:
            return ffn(x_list, takes, out_rows, *weights)
        rows = jnp.concatenate([x[:take] for x, take in zip(x_list, takes)], axis=0)
        rows = lax.all_gather(rows, "ep", axis_index_groups=holders, tiled=True)
        (part,) = ffn([rows], [rows.shape[0]], [rows.shape[0]], *weights)
        part = lax.all_to_all(part, "ep", 0, 0, axis_index_groups=holders, tiled=True)
        part = part.reshape(shards, -1, width).astype(jnp.float32)
        part = jnp.sum(part, axis=0).astype(jnp.bfloat16)
        return jnp.split(part, [sum(out_rows[: i + 1]) for i in range(len(out_rows) - 1)], axis=0)

    vectors = jnp.concatenate(
        [norm_gain, route_ids.reshape(count).astype(jnp.float32), route_gates.reshape(count)]
    ).reshape(1, -1)
    *sent, slot_row, gates_row = prepare(tokens, vectors, shards)
    sent = {name: block for (_, _, name), block in zip(BLOCKS, sent)}

    def move(name, block):
        return across(block, 2 * name[1] if name[0] == "p" else name[1])

    early, late = (
        [("p", m) for m in pairs] + [("s", k) for k in singles]
        for pairs, singles in zip(PAIRED, SINGLE)
    )
    held = {name: move(name, sent[name]) for name in early}
    later = after([sent[name] for name in late], [held[early[0]]])
    held.update({name: move(name, block) for name, block in zip(late, later)})
    back = {}
    for group in (early, late):
        pairs = [name for name in group if name[0] == "p"]
        singles = [name for name in group if name[0] == "s"]
        blocks = [held[name] for name in pairs]
        first = [held[name] for name in singles] if group is early else []
        swapped = across(second_halves(blocks, first), 1)
        own, other, *results = expert(blocks, swapped, [held[name] for name in singles])
        waits = [held[name] for name in FORWARD] if group is early else [back[name] for name in RETURN]
        if group is early:
            (other,) = after([other], waits)
        else:
            other, *results = after([other] + results, waits)
        blocks = dict(zip(singles, results))
        blocks.update(zip(pairs, zipped(own, across(other, 1))))
        back.update({name: move(name, blocks[name]) for name in group})
    return combine(tokens, slot_row, gates_row, [back[name] for _, _, name in BLOCKS])


def solution(mesh):
    in_specs = (
        P(("groups", "ep"), None),
        P(),
        P(None, "ep"),
        P(None, "ep"),
        P("ep", None),
        P(("groups", "ep"), None),
        P(("groups", "ep"), None),
    )
    out_specs = P(("groups", "ep"), None)
    return jax.shard_map(
        per_device, mesh=mesh, in_specs=in_specs, out_specs=out_specs, check_vma=False
    )
```

```python
import functools

import jax
import jax.numpy as jnp
from jax import lax
from jax.experimental import pallas as pl
from jax.experimental.pallas import tpu as pltpu
from jax.sharding import PartitionSpec as P

EXPERTS = 16
CAP = 8
PAIRS = EXPERTS // 2
PAIRED = ((4, 2, 3, 0), (5, 1))
SINGLE = ((12, 13), (14, 15))
BLOCKS = sorted(
    [(2 * m, 2, ("p", m)) for group in PAIRED for m in group]
    + [(k, 1, ("s", k)) for group in SINGLE for k in group]
)
FORWARD = (("p", 5), ("p", 1), ("s", 14), ("s", 15))
RETURN = (("p", 2), ("s", 12), ("p", 4))
RING = 3
SPLIT = 2
PREP_VMEM = 51 * 2**20
HBM = pl.BlockSpec(memory_space=pltpu.HBM)
VMEM = pl.BlockSpec(memory_space=pltpu.VMEM)


def tile_of(extent, most):
    size = min(most, extent)
    while extent % size:
        size -= 128
    return size


def turned(values, axis):
    count = max(values.shape)
    spread = jnp.broadcast_to(values, (count, count))
    row_at = lax.broadcasted_iota(jnp.int32, (count, count), 0)
    column_at = lax.broadcasted_iota(jnp.int32, (count, count), 1)
    return jnp.sum(jnp.where(row_at == column_at, spread, 0.0), axis=axis, keepdims=True)


def ranks(ids_row, axis):
    count = ids_row.shape[1]
    row_at = lax.broadcasted_iota(jnp.int32, (count, count), 0)
    column_at = lax.broadcasted_iota(jnp.int32, (count, count), 1)
    same = turned(ids_row, 1) == ids_row
    before = row_at < column_at if axis == 0 else column_at < row_at
    return jnp.sum(jnp.where(same & before, 1.0, 0.0), axis=axis, keepdims=True)


def prep_kernel(shards, tokens_hbm, vectors_ref, *refs):
    out_refs = refs[: len(BLOCKS)]
    slot_ref, gate_ref, tokens_ref, sems = refs[len(BLOCKS) :]
    count, width = tokens_ref.shape
    chunk = tile_of(width, 1024)
    starts = list(range(0, width, chunk))
    copies = [
        pltpu.make_async_copy(
            tokens_hbm.at[:, pl.ds(at, chunk)], tokens_ref.at[:, pl.ds(at, chunk)], sems.at[i]
        )
        for i, at in enumerate(starts)
    ]
    for copy in copies:
        copy.start()
    mine = lax.axis_index("ep") // shards
    ids_row = vectors_ref[:, width : width + count].astype(jnp.int32)
    rank_row = ranks(ids_row.astype(jnp.float32), 0).astype(jnp.int32)
    slot_row = (ids_row ^ mine) * CAP + rank_row
    slots = EXPERTS * CAP
    pick = (lax.broadcasted_iota(jnp.int32, (slots, count), 0) == slot_row).astype(jnp.bfloat16)
    slot_ref[...] = jnp.broadcast_to(slot_row, slot_ref.shape)
    gate_ref[...] = jnp.broadcast_to(vectors_ref[:, width + count :], gate_ref.shape)
    square_sum = jnp.zeros((count, 128), jnp.float32)
    for first, copy in zip(starts, copies):
        copy.wait()
        for lane in range(first, first + chunk, 128):
            wide = tokens_ref[:, lane : lane + 128].astype(jnp.float32)
            square_sum = square_sum + wide * wide
    scale = lax.rsqrt(jnp.sum(square_sum, axis=1, keepdims=True) / width + 1e-05)
    for first in starts:
        part = slice(first, first + chunk)
        wide = tokens_ref[:, part].astype(jnp.float32)
        normed = (wide * scale * vectors_ref[:, part]).astype(jnp.bfloat16)
        rows = jnp.dot(pick, normed, preferred_element_type=jnp.float32)
        for (k, size, _), out_ref in zip(BLOCKS, out_refs):
            out_ref[:, part] = rows[k * CAP : (k + size) * CAP].astype(jnp.bfloat16)


def prepare(tokens, vectors, shards):
    count, width = tokens.shape
    return pl.pallas_call(
        functools.partial(prep_kernel, shards),
        in_specs=[HBM, VMEM],
        out_shape=[
            jax.ShapeDtypeStruct((size * CAP, width), jnp.bfloat16) for _, size, _ in BLOCKS
        ]
        + [
            jax.ShapeDtypeStruct((8, count), jnp.int32),
            jax.ShapeDtypeStruct((8, count), jnp.float32),
        ],
        scratch_shapes=[
            pltpu.VMEM((count, width), jnp.bfloat16),
            pltpu.SemaphoreType.DMA((width // tile_of(width, 1024),)),
        ],
        compiler_params=pltpu.CompilerParams(vmem_limit_bytes=PREP_VMEM),
        cost_estimate=pl.CostEstimate(
            flops=2 * count * count * width, bytes_accessed=4 * count * width, transcendentals=0
        ),
        name="prepare",
    )(tokens, vectors)


def halves_kernel(count, *refs):
    out_ref = refs[-1]
    width = out_ref.shape[1]
    chunk = tile_of(width, 1024)
    for first in range(0, width, chunk):
        part = slice(first, first + chunk)
        out_ref[:, part] = jnp.concatenate(
            [ref[:, part].astype(jnp.float32)[CAP:] for ref in refs[:count]], axis=0
        ).astype(jnp.bfloat16)


def second_halves(blocks, waits=()):
    width = blocks[0].shape[1]
    return pl.pallas_call(
        functools.partial(halves_kernel, len(blocks)),
        in_specs=[VMEM] * len(blocks) + [VMEM] * len(waits),
        out_specs=VMEM,
        out_shape=jax.ShapeDtypeStruct((CAP * len(blocks), width), jnp.bfloat16),
        compiler_params=pltpu.CompilerParams(vmem_limit_bytes=12 * 2**20),
        cost_estimate=pl.CostEstimate(
            flops=0, bytes_accessed=4 * CAP * len(blocks) * width, transcendentals=0
        ),
        name="second_halves",
    )(*blocks, *waits)


def zip_kernel(waits, upper_ref, lower_ref, *refs):
    out_refs = refs[waits:]
    width = upper_ref.shape[1]
    chunk = tile_of(width, 1024)
    for first in range(0, width, chunk):
        part = slice(first, first + chunk)
        upper = upper_ref[:, part].astype(jnp.float32)
        lower = lower_ref[:, part].astype(jnp.float32)
        for k, out_ref in enumerate(out_refs):
            rows = slice(k * CAP, (k + 1) * CAP)
            both = jnp.concatenate([upper[rows], lower[rows]], axis=0)
            out_ref[:, part] = both.astype(jnp.bfloat16)


def zipped(upper, lower, waits=()):
    rows, width = upper.shape
    return pl.pallas_call(
        functools.partial(zip_kernel, len(waits)),
        in_specs=[VMEM] * 2 + [VMEM] * len(waits),
        out_specs=[VMEM] * (rows // CAP),
        out_shape=[jax.ShapeDtypeStruct((2 * CAP, width), jnp.bfloat16)] * (rows // CAP),
        compiler_params=pltpu.CompilerParams(vmem_limit_bytes=12 * 2**20),
        cost_estimate=pl.CostEstimate(flops=0, bytes_accessed=8 * rows * width, transcendentals=0),
        name="zipped",
    )(upper, lower, *waits)


def after_kernel(count, *refs):
    for block_ref, out_ref in zip(refs[:count], refs[-count:]):
        out_ref[...] = block_ref[...]


def after(blocks, waits):
    count = len(blocks)
    return pl.pallas_call(
        functools.partial(after_kernel, count),
        in_specs=[VMEM] * (count + len(waits)),
        out_specs=[VMEM] * count,
        out_shape=[jax.ShapeDtypeStruct(block.shape, block.dtype) for block in blocks],
        compiler_params=pltpu.CompilerParams(vmem_limit_bytes=12 * 2**20),
        cost_estimate=pl.CostEstimate(flops=0, bytes_accessed=0, transcendentals=0),
        name="after",
    )(*blocks, *waits)


def ffn_kernel(takes, outs, gate_hbm, up_hbm, down_hbm, *refs):
    parts = len(takes)
    x_refs, out_refs = refs[:parts], refs[parts : parts + outs]
    x_all, gate_sum, up_sum, hidden, gate_ring, up_ring, down_ring, sems = refs[
        parts + outs :
    ]
    depth, columns = gate_ring.shape[1], down_ring.shape[2]
    width = x_all.shape[1]
    up_steps, down_steps = width // depth, width // columns
    ahead = min(RING, up_steps)
    down_ahead = min(RING, down_steps)

    def up_copies(step):
        slot = lax.rem(step, RING)
        share = depth // SPLIT
        copies = []
        for part in range(SPLIT):
            rows = pl.ds(pl.multiple_of(step * depth + part * share, share), share)
            to = pl.ds(part * share, share)
            for i, (hbm, ring) in enumerate(((gate_hbm, gate_ring), (up_hbm, up_ring))):
                copies.append(
                    pltpu.make_async_copy(hbm.at[rows], ring.at[slot, to], sems.at[i, slot, part])
                )
        return copies

    def down_copies(step):
        slot = lax.rem(step, RING)
        cols = pl.ds(pl.multiple_of(step * columns, columns), columns)
        share = down_ring.shape[1] // SPLIT
        return [
            pltpu.make_async_copy(
                down_hbm.at[pl.ds(part * share, share), cols],
                down_ring.at[slot, pl.ds(part * share, share)],
                sems.at[2, slot, part],
            )
            for part in range(SPLIT)
        ]

    for step in range(ahead):
        for copy in up_copies(step):
            copy.start()
    for step in range(down_ahead):
        for copy in down_copies(step):
            copy.start()
    for first in range(0, width, depth):
        x_all[:, first : first + depth] = jnp.concatenate(
            [
                ref[:, first : first + depth].astype(jnp.float32)[:take]
                for ref, take in zip(x_refs, takes)
            ],
            axis=0,
        ).astype(jnp.bfloat16)
    gate_sum[...] = jnp.zeros_like(gate_sum)
    up_sum[...] = jnp.zeros_like(up_sum)

    def up_step(step, carry):
        for copy in up_copies(step):
            copy.wait()
        slot = lax.rem(step, RING)
        x = x_all[:, pl.ds(pl.multiple_of(step * depth, depth), depth)]
        gate_sum[...] += jnp.dot(x, gate_ring[slot], preferred_element_type=jnp.float32)
        up_sum[...] += jnp.dot(x, up_ring[slot], preferred_element_type=jnp.float32)

        @pl.when(step + RING < up_steps)
        def _():
            for copy in up_copies(step + RING):
                copy.start()

        return carry

    lax.fori_loop(0, up_steps, up_step, 0)
    gate = gate_sum[...]
    hidden[...] = (gate / (1.0 + jnp.exp(-gate)) * up_sum[...]).astype(jnp.bfloat16)

    def down_step(step, carry):
        for copy in down_copies(step):
            copy.wait()
        part = jnp.dot(
            hidden[...], down_ring[lax.rem(step, RING)], preferred_element_type=jnp.float32
        )
        at = pl.ds(pl.multiple_of(step * columns, columns), columns)
        low = 0
        for out_ref in out_refs:
            rows = out_ref.shape[0]
            out_ref[:, at] = part[low : low + rows].astype(jnp.bfloat16)
            low += rows

        @pl.when(step + RING < down_steps)
        def _():
            for copy in down_copies(step + RING):
                copy.start()

        return carry

    lax.fori_loop(0, down_steps, down_step, 0)


def ffn(x_list, takes, out_rows, gate, up, down):
    parts = len(x_list)
    width = x_list[0].shape[1]
    units = gate.shape[1]
    depth = tile_of(width, 1024)
    columns = tile_of(width, 1024)
    total = sum(takes)
    return pl.pallas_call(
        functools.partial(ffn_kernel, takes, len(out_rows)),
        in_specs=[HBM] * 3 + [VMEM] * parts,
        out_specs=[VMEM] * len(out_rows),
        out_shape=[jax.ShapeDtypeStruct((rows, width), jnp.bfloat16) for rows in out_rows],
        scratch_shapes=[
            pltpu.VMEM((total, width), jnp.bfloat16),
            pltpu.VMEM((total, units), jnp.float32),
            pltpu.VMEM((total, units), jnp.float32),
            pltpu.VMEM((total, units), jnp.bfloat16),
            pltpu.VMEM((RING, depth, units), jnp.bfloat16),
            pltpu.VMEM((RING, depth, units), jnp.bfloat16),
            pltpu.VMEM((RING, units, columns), jnp.bfloat16),
            pltpu.SemaphoreType.DMA((3, RING, SPLIT)),
        ],
        compiler_params=pltpu.CompilerParams(vmem_limit_bytes=50 * 2**20),
        cost_estimate=pl.CostEstimate(
            flops=6 * total * width * units,
            bytes_accessed=6 * width * units + 4 * total * width,
            transcendentals=total * units,
        ),
        name="ffn",
    )(gate, up, down, *x_list)


def combine_kernel(tokens_ref, slot_ref, gates_ref, *refs):
    back_refs, out_hbm, staged, sems = refs[:-3], refs[-3], refs[-2], refs[-1]
    count, width = tokens_ref.shape
    chunk = tile_of(width, 1024)
    slot = turned(slot_ref[0:1].astype(jnp.float32), 1).astype(jnp.int32)
    gates = turned(gates_ref[0:1], 1)
    slots = EXPERTS * CAP
    table = (lax.broadcasted_iota(jnp.int32, (count, slots), 1) == slot).astype(jnp.bfloat16)
    copies = []
    for i, first in enumerate(range(0, width, chunk)):
        part = slice(first, first + chunk)
        back = jnp.concatenate(
            [ref[:, part].astype(jnp.float32) for ref in back_refs], axis=0
        ).astype(jnp.bfloat16)
        summed = jnp.dot(table, back, preferred_element_type=jnp.float32)
        wide = tokens_ref[:, part].astype(jnp.float32)
        staged[:, part] = (wide + gates * summed).astype(jnp.bfloat16)
        copies.append(
            pltpu.make_async_copy(
                staged.at[:, pl.ds(first, chunk)], out_hbm.at[:, pl.ds(first, chunk)], sems.at[i]
            )
        )
        copies[-1].start()
    for copy in copies:
        copy.wait()


def combine(tokens, slot_row, gates_row, back_list):
    count, width = tokens.shape
    return pl.pallas_call(
        combine_kernel,
        in_specs=[VMEM] * (3 + len(back_list)),
        out_specs=HBM,
        out_shape=jax.ShapeDtypeStruct((count, width), jnp.bfloat16),
        scratch_shapes=[
            pltpu.VMEM((count, width), jnp.bfloat16),
            pltpu.SemaphoreType.DMA((width // tile_of(width, 1024),)),
        ],
        compiler_params=pltpu.CompilerParams(vmem_limit_bytes=16 * 2**20),
        cost_estimate=pl.CostEstimate(
            flops=2 * count * count * width, bytes_accessed=6 * count * width, transcendentals=0
        ),
        name="combine",
    )(tokens, slot_row, gates_row, *back_list)


def per_device(tokens, norm_gain, expert_gate, expert_up, expert_down, route_ids, route_gates):
    devices = lax.axis_size("ep")
    shards = devices // EXPERTS
    count, width = tokens.shape
    weights = (expert_gate, expert_up, expert_down)
    holders = [[e * shards + s for s in range(shards)] for e in range(EXPERTS)]

    def across(block, k):
        if k == 0:
            return block
        pairs = [(d, (d // shards ^ k) * shards + d % shards) for d in range(devices)]
        return lax.ppermute(block, "ep", pairs)

    def expert(pairs, swapped, singles):
        half = swapped.shape[0]
        x_list = pairs + [swapped] + singles
        takes = [CAP] * len(pairs) + [half] + [CAP] * len(singles)
        out_rows = [half, half] + [CAP] * len(singles)
        if shards == 1:
            return ffn(x_list, takes, out_rows, *weights)
        rows = jnp.concatenate([x[:take] for x, take in zip(x_list, takes)], axis=0)
        rows = lax.all_gather(rows, "ep", axis_index_groups=holders, tiled=True)
        (part,) = ffn([rows], [rows.shape[0]], [rows.shape[0]], *weights)
        part = lax.all_to_all(part, "ep", 0, 0, axis_index_groups=holders, tiled=True)
        part = part.reshape(shards, -1, width).astype(jnp.float32)
        part = jnp.sum(part, axis=0).astype(jnp.bfloat16)
        return jnp.split(part, [sum(out_rows[: i + 1]) for i in range(len(out_rows) - 1)], axis=0)

    parts = (norm_gain.reshape(1, width), route_ids.reshape(1, count), route_gates.reshape(1, count))
    at = lax.broadcasted_iota(jnp.int32, (1, width + 2 * count), 1)
    gain, ids, gates = (
        jnp.pad(part, ((0, 0), (low, width + 2 * count - low - part.shape[1])))
        for part, low in zip(parts, (0, width, width + count))
    )
    vectors = jnp.where(at < width, gain, jnp.where(at < width + count, ids.astype(jnp.float32), gates))
    *sent, slot_row, gates_row = prepare(tokens, vectors, shards)
    sent = {name: block for (_, _, name), block in zip(BLOCKS, sent)}

    def move(name, block):
        return across(block, 2 * name[1] if name[0] == "p" else name[1])

    early, late = (
        [("p", m) for m in pairs] + [("s", k) for k in singles]
        for pairs, singles in zip(PAIRED, SINGLE)
    )
    held = {name: move(name, sent[name]) for name in early}
    later = after([sent[name] for name in late], [held[early[0]]])
    held.update({name: move(name, block) for name, block in zip(late, later)})
    back = {}
    for group in (early, late):
        pairs = [name for name in group if name[0] == "p"]
        singles = [name for name in group if name[0] == "s"]
        blocks = [held[name] for name in pairs]
        first = [held[name] for name in singles] if group is early else []
        swapped = across(second_halves(blocks, first), 1)
        own, other, *results = expert(blocks, swapped, [held[name] for name in singles])
        waits = [held[name] for name in FORWARD] if group is early else [back[name] for name in RETURN]
        if group is early:
            (other,) = after([other], waits)
        else:
            other, *results = after([other] + results, waits)
        blocks = dict(zip(singles, results))
        blocks.update(zip(pairs, zipped(own, across(other, 1))))
        back.update({name: move(name, blocks[name]) for name in group})
    return combine(tokens, slot_row, gates_row, [back[name] for _, _, name in BLOCKS])


def solution(mesh):
    in_specs = (
        P(("groups", "ep"), None),
        P(),
        P(None, "ep"),
        P(None, "ep"),
        P("ep", None),
        P(("groups", "ep"), None),
        P(("groups", "ep"), None),
    )
    out_specs = P(("groups", "ep"), None)
    return jax.shard_map(
        per_device, mesh=mesh, in_specs=in_specs, out_specs=out_specs, check_vma=False
    )
```

```python
import functools

import jax
import jax.numpy as jnp
from jax import lax
from jax.experimental import pallas as pl
from jax.experimental.pallas import tpu as pltpu
from jax.sharding import PartitionSpec as P

EXPERTS = 16
CAP = 8
PAIRS = EXPERTS // 2
PAIRED = ((4, 2, 3, 0), (5, 1))
SINGLE = ((12, 13), (14, 15))
BLOCKS = sorted(
    [(2 * m, 2, ("p", m)) for group in PAIRED for m in group]
    + [(k, 1, ("s", k)) for group in SINGLE for k in group]
)
FORWARD = (("p", 5), ("p", 1), ("s", 14), ("s", 15))
RETURN = (("p", 2), ("s", 12), ("p", 4))
RING = 6
SPLIT = 1
PREP_VMEM = 51 * 2**20
HBM = pl.BlockSpec(memory_space=pltpu.HBM)
VMEM = pl.BlockSpec(memory_space=pltpu.VMEM)


def tile_of(extent, most):
    size = min(most, extent)
    while extent % size:
        size -= 128
    return size


def turned(values, axis):
    count = max(values.shape)
    spread = jnp.broadcast_to(values, (count, count))
    row_at = lax.broadcasted_iota(jnp.int32, (count, count), 0)
    column_at = lax.broadcasted_iota(jnp.int32, (count, count), 1)
    return jnp.sum(jnp.where(row_at == column_at, spread, 0.0), axis=axis, keepdims=True)


def ranks(ids_row, axis):
    count = ids_row.shape[1]
    row_at = lax.broadcasted_iota(jnp.int32, (count, count), 0)
    column_at = lax.broadcasted_iota(jnp.int32, (count, count), 1)
    same = turned(ids_row, 1) == ids_row
    before = row_at < column_at if axis == 0 else column_at < row_at
    return jnp.sum(jnp.where(same & before, 1.0, 0.0), axis=axis, keepdims=True)


def prep_kernel(shards, tokens_hbm, vectors_ref, *refs):
    out_refs = refs[: len(BLOCKS)]
    slot_ref, gate_ref, tokens_ref, sems = refs[len(BLOCKS) :]
    count, width = tokens_ref.shape
    chunk = tile_of(width, 1024)
    starts = list(range(0, width, chunk))
    copies = [
        pltpu.make_async_copy(
            tokens_hbm.at[:, pl.ds(at, chunk)], tokens_ref.at[:, pl.ds(at, chunk)], sems.at[i]
        )
        for i, at in enumerate(starts)
    ]
    for copy in copies:
        copy.start()
    mine = lax.axis_index("ep") // shards
    ids_row = vectors_ref[:, width : width + count].astype(jnp.int32)
    rank_row = ranks(ids_row.astype(jnp.float32), 0).astype(jnp.int32)
    slot_row = (ids_row ^ mine) * CAP + rank_row
    slots = EXPERTS * CAP
    pick = (lax.broadcasted_iota(jnp.int32, (slots, count), 0) == slot_row).astype(jnp.bfloat16)
    slot_ref[...] = jnp.broadcast_to(slot_row, slot_ref.shape)
    gate_ref[...] = jnp.broadcast_to(vectors_ref[:, width + count :], gate_ref.shape)
    square_sum = jnp.zeros((count, 128), jnp.float32)
    for first, copy in zip(starts, copies):
        copy.wait()
        for lane in range(first, first + chunk, 128):
            wide = tokens_ref[:, lane : lane + 128].astype(jnp.float32)
            square_sum = square_sum + wide * wide
    scale = lax.rsqrt(jnp.sum(square_sum, axis=1, keepdims=True) / width + 1e-05)
    for first in starts:
        part = slice(first, first + chunk)
        wide = tokens_ref[:, part].astype(jnp.float32)
        normed = (wide * scale * vectors_ref[:, part]).astype(jnp.bfloat16)
        rows = jnp.dot(pick, normed, preferred_element_type=jnp.float32)
        for (k, size, _), out_ref in zip(BLOCKS, out_refs):
            out_ref[:, part] = rows[k * CAP : (k + size) * CAP].astype(jnp.bfloat16)


def prepare(tokens, vectors, shards):
    count, width = tokens.shape
    return pl.pallas_call(
        functools.partial(prep_kernel, shards),
        in_specs=[HBM, VMEM],
        out_shape=[
            jax.ShapeDtypeStruct((size * CAP, width), jnp.bfloat16) for _, size, _ in BLOCKS
        ]
        + [
            jax.ShapeDtypeStruct((8, count), jnp.int32),
            jax.ShapeDtypeStruct((8, count), jnp.float32),
        ],
        scratch_shapes=[
            pltpu.VMEM((count, width), jnp.bfloat16),
            pltpu.SemaphoreType.DMA((width // tile_of(width, 1024),)),
        ],
        compiler_params=pltpu.CompilerParams(vmem_limit_bytes=PREP_VMEM),
        cost_estimate=pl.CostEstimate(
            flops=2 * count * count * width, bytes_accessed=4 * count * width, transcendentals=0
        ),
        name="prepare",
    )(tokens, vectors)


def halves_kernel(count, *refs):
    out_ref = refs[-1]
    width = out_ref.shape[1]
    chunk = tile_of(width, 1024)
    for first in range(0, width, chunk):
        part = slice(first, first + chunk)
        out_ref[:, part] = jnp.concatenate(
            [ref[:, part].astype(jnp.float32)[CAP:] for ref in refs[:count]], axis=0
        ).astype(jnp.bfloat16)


def second_halves(blocks, waits=()):
    width = blocks[0].shape[1]
    return pl.pallas_call(
        functools.partial(halves_kernel, len(blocks)),
        in_specs=[VMEM] * len(blocks) + [VMEM] * len(waits),
        out_specs=VMEM,
        out_shape=jax.ShapeDtypeStruct((CAP * len(blocks), width), jnp.bfloat16),
        compiler_params=pltpu.CompilerParams(vmem_limit_bytes=12 * 2**20),
        cost_estimate=pl.CostEstimate(
            flops=0, bytes_accessed=4 * CAP * len(blocks) * width, transcendentals=0
        ),
        name="second_halves",
    )(*blocks, *waits)


def zip_kernel(waits, upper_ref, lower_ref, *refs):
    out_refs = refs[waits:]
    width = upper_ref.shape[1]
    chunk = tile_of(width, 1024)
    for first in range(0, width, chunk):
        part = slice(first, first + chunk)
        upper = upper_ref[:, part].astype(jnp.float32)
        lower = lower_ref[:, part].astype(jnp.float32)
        for k, out_ref in enumerate(out_refs):
            rows = slice(k * CAP, (k + 1) * CAP)
            both = jnp.concatenate([upper[rows], lower[rows]], axis=0)
            out_ref[:, part] = both.astype(jnp.bfloat16)


def zipped(upper, lower, waits=()):
    rows, width = upper.shape
    return pl.pallas_call(
        functools.partial(zip_kernel, len(waits)),
        in_specs=[VMEM] * 2 + [VMEM] * len(waits),
        out_specs=[VMEM] * (rows // CAP),
        out_shape=[jax.ShapeDtypeStruct((2 * CAP, width), jnp.bfloat16)] * (rows // CAP),
        compiler_params=pltpu.CompilerParams(vmem_limit_bytes=12 * 2**20),
        cost_estimate=pl.CostEstimate(flops=0, bytes_accessed=8 * rows * width, transcendentals=0),
        name="zipped",
    )(upper, lower, *waits)


def after_kernel(count, *refs):
    for block_ref, out_ref in zip(refs[:count], refs[-count:]):
        out_ref[...] = block_ref[...]


def after(blocks, waits):
    count = len(blocks)
    return pl.pallas_call(
        functools.partial(after_kernel, count),
        in_specs=[VMEM] * (count + len(waits)),
        out_specs=[VMEM] * count,
        out_shape=[jax.ShapeDtypeStruct(block.shape, block.dtype) for block in blocks],
        compiler_params=pltpu.CompilerParams(vmem_limit_bytes=12 * 2**20),
        cost_estimate=pl.CostEstimate(flops=0, bytes_accessed=0, transcendentals=0),
        name="after",
    )(*blocks, *waits)


def ffn_kernel(takes, outs, gate_hbm, up_hbm, down_hbm, *refs):
    parts = len(takes)
    x_refs, out_refs = refs[:parts], refs[parts : parts + outs]
    x_all, gate_sum, up_sum, hidden, gate_ring, up_ring, down_ring, sems = refs[
        parts + outs :
    ]
    depth, columns = gate_ring.shape[1], down_ring.shape[2]
    width = x_all.shape[1]
    up_steps, down_steps = width // depth, width // columns
    ahead = min(RING, up_steps)
    down_ahead = min(RING, down_steps)

    def up_copies(step):
        slot = lax.rem(step, RING)
        share = depth // SPLIT
        copies = []
        for part in range(SPLIT):
            rows = pl.ds(pl.multiple_of(step * depth + part * share, share), share)
            to = pl.ds(part * share, share)
            for i, (hbm, ring) in enumerate(((gate_hbm, gate_ring), (up_hbm, up_ring))):
                copies.append(
                    pltpu.make_async_copy(hbm.at[rows], ring.at[slot, to], sems.at[i, slot, part])
                )
        return copies

    def down_copies(step):
        slot = lax.rem(step, RING)
        cols = pl.ds(pl.multiple_of(step * columns, columns), columns)
        share = down_ring.shape[1] // SPLIT
        return [
            pltpu.make_async_copy(
                down_hbm.at[pl.ds(part * share, share), cols],
                down_ring.at[slot, pl.ds(part * share, share)],
                sems.at[2, slot, part],
            )
            for part in range(SPLIT)
        ]

    for step in range(ahead):
        for copy in up_copies(step):
            copy.start()
    for step in range(down_ahead):
        for copy in down_copies(step):
            copy.start()
    for first in range(0, width, depth):
        x_all[:, first : first + depth] = jnp.concatenate(
            [
                ref[:, first : first + depth].astype(jnp.float32)[:take]
                for ref, take in zip(x_refs, takes)
            ],
            axis=0,
        ).astype(jnp.bfloat16)
    gate_sum[...] = jnp.zeros_like(gate_sum)
    up_sum[...] = jnp.zeros_like(up_sum)

    def up_step(step, carry):
        for copy in up_copies(step):
            copy.wait()
        slot = lax.rem(step, RING)
        x = x_all[:, pl.ds(pl.multiple_of(step * depth, depth), depth)]
        gate_sum[...] += jnp.dot(x, gate_ring[slot], preferred_element_type=jnp.float32)
        up_sum[...] += jnp.dot(x, up_ring[slot], preferred_element_type=jnp.float32)

        @pl.when(step + RING < up_steps)
        def _():
            for copy in up_copies(step + RING):
                copy.start()

        return carry

    lax.fori_loop(0, up_steps, up_step, 0)
    gate = gate_sum[...]
    hidden[...] = (gate / (1.0 + jnp.exp(-gate)) * up_sum[...]).astype(jnp.bfloat16)

    def down_step(step, carry):
        for copy in down_copies(step):
            copy.wait()
        part = jnp.dot(
            hidden[...], down_ring[lax.rem(step, RING)], preferred_element_type=jnp.float32
        )
        at = pl.ds(pl.multiple_of(step * columns, columns), columns)
        low = 0
        for out_ref in out_refs:
            rows = out_ref.shape[0]
            out_ref[:, at] = part[low : low + rows].astype(jnp.bfloat16)
            low += rows

        @pl.when(step + RING < down_steps)
        def _():
            for copy in down_copies(step + RING):
                copy.start()

        return carry

    lax.fori_loop(0, down_steps, down_step, 0)


def ffn(x_list, takes, out_rows, gate, up, down):
    parts = len(x_list)
    width = x_list[0].shape[1]
    units = gate.shape[1]
    depth = tile_of(width, 512)
    columns = tile_of(width, 512)
    total = sum(takes)
    return pl.pallas_call(
        functools.partial(ffn_kernel, takes, len(out_rows)),
        in_specs=[HBM] * 3 + [VMEM] * parts,
        out_specs=[VMEM] * len(out_rows),
        out_shape=[jax.ShapeDtypeStruct((rows, width), jnp.bfloat16) for rows in out_rows],
        scratch_shapes=[
            pltpu.VMEM((total, width), jnp.bfloat16),
            pltpu.VMEM((total, units), jnp.float32),
            pltpu.VMEM((total, units), jnp.float32),
            pltpu.VMEM((total, units), jnp.bfloat16),
            pltpu.VMEM((RING, depth, units), jnp.bfloat16),
            pltpu.VMEM((RING, depth, units), jnp.bfloat16),
            pltpu.VMEM((RING, units, columns), jnp.bfloat16),
            pltpu.SemaphoreType.DMA((3, RING, SPLIT)),
        ],
        compiler_params=pltpu.CompilerParams(vmem_limit_bytes=50 * 2**20),
        cost_estimate=pl.CostEstimate(
            flops=6 * total * width * units,
            bytes_accessed=6 * width * units + 4 * total * width,
            transcendentals=total * units,
        ),
        name="ffn",
    )(gate, up, down, *x_list)


def combine_kernel(tokens_ref, slot_ref, gates_ref, *refs):
    back_refs, out_hbm, staged, sems = refs[:-3], refs[-3], refs[-2], refs[-1]
    count, width = tokens_ref.shape
    chunk = tile_of(width, 1024)
    slot = turned(slot_ref[0:1].astype(jnp.float32), 1).astype(jnp.int32)
    gates = turned(gates_ref[0:1], 1)
    slots = EXPERTS * CAP
    table = (lax.broadcasted_iota(jnp.int32, (count, slots), 1) == slot).astype(jnp.bfloat16)
    copies = []
    for i, first in enumerate(range(0, width, chunk)):
        part = slice(first, first + chunk)
        back = jnp.concatenate(
            [ref[:, part].astype(jnp.float32) for ref in back_refs], axis=0
        ).astype(jnp.bfloat16)
        summed = jnp.dot(table, back, preferred_element_type=jnp.float32)
        wide = tokens_ref[:, part].astype(jnp.float32)
        staged[:, part] = (wide + gates * summed).astype(jnp.bfloat16)
        copies.append(
            pltpu.make_async_copy(
                staged.at[:, pl.ds(first, chunk)], out_hbm.at[:, pl.ds(first, chunk)], sems.at[i]
            )
        )
        copies[-1].start()
    for copy in copies:
        copy.wait()


def combine(tokens, slot_row, gates_row, back_list):
    count, width = tokens.shape
    return pl.pallas_call(
        combine_kernel,
        in_specs=[VMEM] * (3 + len(back_list)),
        out_specs=HBM,
        out_shape=jax.ShapeDtypeStruct((count, width), jnp.bfloat16),
        scratch_shapes=[
            pltpu.VMEM((count, width), jnp.bfloat16),
            pltpu.SemaphoreType.DMA((width // tile_of(width, 1024),)),
        ],
        compiler_params=pltpu.CompilerParams(vmem_limit_bytes=16 * 2**20),
        cost_estimate=pl.CostEstimate(
            flops=2 * count * count * width, bytes_accessed=6 * count * width, transcendentals=0
        ),
        name="combine",
    )(tokens, slot_row, gates_row, *back_list)


def per_device(tokens, norm_gain, expert_gate, expert_up, expert_down, route_ids, route_gates):
    devices = lax.axis_size("ep")
    shards = devices // EXPERTS
    count, width = tokens.shape
    weights = (expert_gate, expert_up, expert_down)
    holders = [[e * shards + s for s in range(shards)] for e in range(EXPERTS)]

    def across(block, k):
        if k == 0:
            return block
        pairs = [(d, (d // shards ^ k) * shards + d % shards) for d in range(devices)]
        return lax.ppermute(block, "ep", pairs)

    def expert(pairs, swapped, singles):
        half = swapped.shape[0]
        x_list = pairs + [swapped] + singles
        takes = [CAP] * len(pairs) + [half] + [CAP] * len(singles)
        out_rows = [half, half] + [CAP] * len(singles)
        if shards == 1:
            return ffn(x_list, takes, out_rows, *weights)
        rows = jnp.concatenate([x[:take] for x, take in zip(x_list, takes)], axis=0)
        rows = lax.all_gather(rows, "ep", axis_index_groups=holders, tiled=True)
        (part,) = ffn([rows], [rows.shape[0]], [rows.shape[0]], *weights)
        part = lax.all_to_all(part, "ep", 0, 0, axis_index_groups=holders, tiled=True)
        part = part.reshape(shards, -1, width).astype(jnp.float32)
        part = jnp.sum(part, axis=0).astype(jnp.bfloat16)
        return jnp.split(part, [sum(out_rows[: i + 1]) for i in range(len(out_rows) - 1)], axis=0)

    parts = (norm_gain.reshape(1, width), route_ids.reshape(1, count), route_gates.reshape(1, count))
    at = lax.broadcasted_iota(jnp.int32, (1, width + 2 * count), 1)
    gain, ids, gates = (
        jnp.pad(part, ((0, 0), (low, width + 2 * count - low - part.shape[1])))
        for part, low in zip(parts, (0, width, width + count))
    )
    vectors = jnp.where(at < width, gain, jnp.where(at < width + count, ids.astype(jnp.float32), gates))
    *sent, slot_row, gates_row = prepare(tokens, vectors, shards)
    sent = {name: block for (_, _, name), block in zip(BLOCKS, sent)}

    def move(name, block):
        return across(block, 2 * name[1] if name[0] == "p" else name[1])

    early, late = (
        [("p", m) for m in pairs] + [("s", k) for k in singles]
        for pairs, singles in zip(PAIRED, SINGLE)
    )
    held = {name: move(name, sent[name]) for name in early}
    later = after([sent[name] for name in late], [held[early[0]]])
    held.update({name: move(name, block) for name, block in zip(late, later)})
    back = {}
    for group in (early, late):
        pairs = [name for name in group if name[0] == "p"]
        singles = [name for name in group if name[0] == "s"]
        blocks = [held[name] for name in pairs]
        first = [held[name] for name in singles] if group is early else []
        swapped = across(second_halves(blocks, first), 1)
        own, other, *results = expert(blocks, swapped, [held[name] for name in singles])
        waits = [held[name] for name in FORWARD] if group is early else [back[name] for name in RETURN]
        if group is early:
            (other,) = after([other], waits)
        else:
            other, *results = after([other] + results, waits)
        blocks = dict(zip(singles, results))
        blocks.update(zip(pairs, zipped(own, across(other, 1))))
        back.update({name: move(name, blocks[name]) for name in group})
    return combine(tokens, slot_row, gates_row, [back[name] for _, _, name in BLOCKS])


def solution(mesh):
    in_specs = (
        P(("groups", "ep"), None),
        P(),
        P(None, "ep"),
        P(None, "ep"),
        P("ep", None),
        P(("groups", "ep"), None),
        P(("groups", "ep"), None),
    )
    out_specs = P(("groups", "ep"), None)
    return jax.shard_map(
        per_device, mesh=mesh, in_specs=in_specs, out_specs=out_specs, check_vma=False
    )
```
